128 devices in a mesh: edge: 8 (over x, y_lo), feat: 16 (over z, y_hi, core).
Axes of the slice: x: 4, y: 4 (y_hi: 2, y_lo: 2; y = y_hi * 2 + y_lo), z: 4, core: 2. Of those that a mesh axis runs over, the one named last changes fastest.
Arguments:
- grad_out: bfloat16 [262144, 256], P(('edge', 'feat')), may hold values from -6 to 6
- pre_act: bfloat16 [262144, 256], P(('edge', 'feat')), may hold values from -6 to 6
- feat_t: bfloat16 [128, 262144], P('feat', 'edge'), may hold values from -6 to 6
- agg_t: bfloat16 [128, 262144], P('feat', 'edge'), may hold values from -6 to 6
- w_self: bfloat16 [128, 256], replicated, may hold values from -0.375 to 0.375
- w_neigh: bfloat16 [128, 256], replicated, may hold values from -0.375 to 0.375
- blocks: bfloat16 [16384, 4096], P('edge'), may hold values from 0 to 0.029907227
- row_index: int32 [16384], P('edge'), may hold values from 0 to 511, as said below
- col_index: int32 [16384], P('edge'), may hold values from 0 to 4095
- counts: int32 [8], P('edge'), may hold values from 512 to 2048, as said below
Outputs:
- grad_feat_t: bfloat16 [128, 262144], P('feat', 'edge')
- grad_w_self: float32 [128, 256], P('feat')
- grad_w_neigh: float32 [128, 256], P('feat')
The draws below stay inside these ranges and needn't reach their ends.
Inputs may be any that keep to these rules, and one draw needn't show every extreme that they name: `counts`: slots at or after a partition's count hold arbitrary indices and values and are ignored; some partition is full in every draw. `row_index`: indices are local to the slab of the slot's partition.
All inputs are finite; a program needn't handle non-finite values.
Results may differ from the reference program's by a relative error of at most 0.0075.
Values may be sent and summed in bfloat16 or wider, within the bound.
A program may use at most 192 MiB of HBM per device.

```python
import jax
import jax.numpy as jnp
from jax import lax

FIN = 128
HID = 256
BLK = 64
NBP = 2048
SLAB = 32768
NODES = 262144
N_EDGE = 8


def draw_counts(key, part):
    key = jax.random.fold_in(key, 11)
    first_key, second_key = jax.random.split(key)
    groups = NODES // SLAB
    values = jax.random.randint(first_key, (groups,), NBP // 4, NBP + 1)
    fullest = jax.random.randint(second_key, (), 0, groups)
    return jnp.where(jnp.arange(groups) == fullest, NBP, values).astype(jnp.int32)


def draw_row_index(key, part):
    key = jax.random.fold_in(key, 23)
    return jax.random.randint(key, (NODES // SLAB * NBP,), 0, SLAB // 64).astype(jnp.int32)


def draw_col_index(key, part):
    key = jax.random.fold_in(key, 37)
    return jax.random.randint(key, (NODES // SLAB * NBP,), 0, NODES // 64).astype(jnp.int32)


def block_scale(key, extent, pieces, least, high):
    def one(axis_at, shards_of):
        steps = jax.random.uniform(jax.random.fold_in(jax.random.fold_in(key, 6), axis_at), (shards_of,), jnp.float32, least / len(pieces), high / len(pieces))
        return jnp.repeat(jnp.exp(steps), extent[axis_at] // shards_of).reshape((-1,) + (1,) * (len(extent) - axis_at - 1))

    level = one(*pieces[0])
    for cut in pieces[1:]:
        level = level * one(*cut)
    return level


def noise(stream_key, shape, deviation, most, shards=(), kind=jnp.bfloat16):
    drawn = jax.random.normal(stream_key, shape, jnp.float32) * deviation
    if len(shards) > 0:
        drawn = block_scale(stream_key, shape, shards, -0.22, 0.18) * drawn
    return jnp.clip(drawn, min=-most, max=most).astype(kind)


def setup_inputs(seed: int = 0) -> dict:
    key_list = jax.random.split(jax.random.key(seed), 11)
    grad_out = noise(key_list[0], (NODES, HID), 1.0, 6.0, ((0, 128),))
    pre_act = noise(key_list[1], (NODES, HID), 1.0, 6.0, ((0, 128),))
    feat_t = noise(key_list[2], (FIN, NODES), 1.0, 6.0, ((0, 16), (1, 8)))
    agg_t = noise(key_list[3], (FIN, NODES), 1.0, 6.0, ((0, 16), (1, 8)))
    w_self = noise(key_list[4], (FIN, HID), HID ** -0.5, 0.375)
    w_neigh = noise(key_list[5], (FIN, HID), HID ** -0.5, 0.375)
    blocks = jnp.clip(0.029907227 * jax.random.uniform(key_list[6], (N_EDGE * NBP, BLK * BLK), jnp.float32) ** block_scale(key_list[6], (N_EDGE * NBP, BLK * BLK), ((0, 8),), -0.2, 0.2), 0.0, 0.029907227).astype(jnp.bfloat16)
    row_index = draw_row_index(jax.random.fold_in(key_list[10], 71), 0)
    col_index = draw_col_index(jax.random.fold_in(key_list[10], 71), 0)
    counts = draw_counts(jax.random.fold_in(key_list[10], 71), 0)
    return dict(grad_out=grad_out, pre_act=pre_act, feat_t=feat_t, agg_t=agg_t, w_self=w_self, w_neigh=w_neigh, blocks=blocks, row_index=row_index, col_index=col_index, counts=counts)


def reference(grad_out, pre_act, feat_t, agg_t, w_self, w_neigh, blocks, row_index, col_index, counts):
    masked = jnp.where(pre_act > 0, grad_out, jnp.zeros_like(grad_out))
    factor = 1.0 / (NODES ** 0.5)
    grad_w_self = jnp.dot(feat_t, masked, preferred_element_type=jnp.float32) * factor
    grad_w_neigh = jnp.dot(agg_t, masked, preferred_element_type=jnp.float32) * factor
    back_self = jnp.dot(w_self, masked.T, preferred_element_type=jnp.float32).astype(jnp.bfloat16)
    back_neigh = jnp.dot(w_neigh, masked.T, preferred_element_type=jnp.float32).astype(jnp.bfloat16)
    node_blocks = back_neigh.reshape(FIN, NODES // BLK, BLK).transpose(1, 0, 2)
    groups = NODES // SLAB

    def one_partition(totals, group_index):
        first = group_index * NBP
        rows_here = lax.dynamic_slice_in_dim(row_index, first, NBP) + group_index * (SLAB // BLK)
        cols_here = lax.dynamic_slice_in_dim(col_index, first, NBP)
        values = lax.dynamic_slice_in_dim(blocks, first, NBP, 0).astype(jnp.float32).reshape(NBP, BLK, BLK)
        gathered = jnp.take(node_blocks, rows_here, axis=0).astype(jnp.float32)
        product = jnp.einsum("sfi,sij->sfj", gathered, values)
        live = jnp.arange(NBP, dtype=jnp.int32) < counts[group_index]
        product = jnp.where(live[:, None, None], product, jnp.float32(0.0))
        partial_sum = jnp.zeros_like(totals).at[cols_here].add(product)
        rounded = lax.optimization_barrier(partial_sum.astype(jnp.bfloat16))
        return totals + rounded.astype(jnp.float32), None

    start = jnp.zeros((NODES // BLK, FIN, BLK), jnp.float32)
    totals, unused = lax.scan(one_partition, start, jnp.arange(groups, dtype=jnp.int32))
    spread = totals.transpose(1, 0, 2).reshape(FIN, NODES)
    grad_feat_t = (back_self.astype(jnp.float32) + spread).astype(jnp.bfloat16)
    return grad_feat_t, grad_w_self, grad_w_neigh
```

```python
import functools
import math

import jax
import jax.numpy as jnp
from jax import lax
from jax.experimental import pallas as pl
from jax.experimental.pallas import tpu as pltpu
from jax.sharding import PartitionSpec as P

MESH = pl.DeviceIdType.MESH
MIB = 2**20
F32 = jnp.float32
BF16 = jnp.bfloat16
HIGH = dict(preferred_element_type=F32)
NT = (((1,), (1,)), ((), ()))


def masked_rows(grad_ref, pre_ref):
    return jnp.where(pre_ref[...] > 0, grad_ref[...], jnp.zeros_like(grad_ref))


def halves_of(product, owner, out_ref):
    nodes = product.shape[1]
    rows = product[owner * 8 : owner * 8 + 8]
    both = jnp.concatenate([rows[:, : nodes // 2], rows[:, nodes // 2 :]], 0)
    out_ref[owner] = both.astype(BF16)


def neigh_kernel(n_feat, grad_ref, pre_ref, w_ref, out_ref, send, masked, send_sem, recv_sem, own_sem):
    me = lax.axis_index("feat")
    barrier = pltpu.get_barrier_semaphore()
    for k in range(1, n_feat):
        peer = lax.rem(me + k, n_feat)
        pl.semaphore_signal(barrier, inc=1, device_id={"feat": peer}, device_id_type=MESH)

    masked[...] = masked_rows(grad_ref, pre_ref)
    product = lax.dot_general(w_ref[...], masked[...], NT, **HIGH)
    for owner in range(n_feat):
        halves_of(product, owner, send)

    own = pltpu.make_async_copy(send.at[me], out_ref.at[me], own_sem)
    own.start()
    pl.semaphore_wait(barrier, n_feat - 1)

    def copy(peer, slot):
        return pltpu.make_async_remote_copy(
            src_ref=send.at[peer],
            dst_ref=out_ref.at[slot],
            send_sem=send_sem.at[peer],
            recv_sem=recv_sem.at[slot],
            device_id={"feat": peer},
            device_id_type=MESH,
        )

    for k in range(1, n_feat):
        copy(lax.rem(me + k, n_feat), me).start()
    for k in range(1, n_feat):
        copy(lax.rem(me + k, n_feat), me).wait_send()
    for k in range(1, n_feat):
        peer = lax.rem(me + k, n_feat)
        copy(peer, peer).wait_recv()
    own.wait()


def send_neigh(grad_out, pre_act, w_neigh, n_feat):
    nodes, hidden = grad_out.shape
    return pl.pallas_call(
        functools.partial(neigh_kernel, n_feat),
        in_specs=[pl.BlockSpec(memory_space=pltpu.VMEM)] * 3,
        out_specs=pl.BlockSpec(memory_space=pl.ANY),
        out_shape=jax.ShapeDtypeStruct((n_feat, 16, nodes // 2), BF16),
        scratch_shapes=[
            pltpu.VMEM((n_feat, 16, nodes // 2), BF16),
            pltpu.VMEM((nodes, hidden), BF16),
            pltpu.SemaphoreType.DMA((n_feat,)),
            pltpu.SemaphoreType.DMA((n_feat,)),
            pltpu.SemaphoreType.DMA,
        ],
        compiler_params=pltpu.CompilerParams(
            collective_id=0, has_side_effects=True, vmem_limit_bytes=48 * MIB
        ),
        name="send_neigh",
    )(grad_out, pre_act, w_neigh)


def spread_kernel(
    per_step, counts_ref, row_ref, col_ref, neigh_hbm, blocks_hbm, out_hbm,
    neigh, blocks, table, totals, even, odd, packed, neigh_sem, block_sem, out_sem,
):
    steps = blocks.shape[0] // per_step
    pairs = totals.shape[0] - 1
    n_src, _, span = neigh.shape
    n_dest = packed.shape[0]

    def load(i):
        rows = pl.ds(i * per_step, per_step)
        return pltpu.make_async_copy(blocks_hbm.at[rows], blocks.at[rows], block_sem.at[i])

    load_neigh = pltpu.make_async_copy(neigh_hbm, neigh, neigh_sem)
    load_neigh.start()
    for i in range(steps):
        load(i).start()

    @pl.loop(0, pairs // 64)
    def _(i):
        totals[pl.ds(i * 64, 64)] = jnp.zeros((64, 8, 128), F32)

    totals[pairs] = jnp.zeros((8, 128), F32)

    place = lax.broadcasted_iota(jnp.int32, (128, 2048), 1)
    source = place // 1024 * 64 + (place % 512) // 16 * 2 + place // 512 % 2
    node = lax.broadcasted_iota(jnp.int32, (128, 2048), 0)
    permute = jnp.where(source == node, 1.0, 0.0).astype(BF16)
    load_neigh.wait()
    tiles = span // 128

    @pl.loop(0, n_src)
    def _(src):
        x = jnp.concatenate([neigh[src, :, t * 128 : (t + 1) * 128] for t in range(tiles)], 0)
        for b in range(2):
            y = jnp.dot(x, permute[:, b * 1024 : (b + 1) * 1024], **HIGH)
            for t in range(tiles):
                for h in range(2):
                    at = t * 16 + h * 8
                    both = jnp.concatenate([y[at : at + 8, :512], y[at : at + 8, 512:]], 0)
                    table[src * (4 * tiles) + h * 2 * tiles + 2 * t + b] = both.astype(BF16)

    lane = lax.broadcasted_iota(jnp.int32, (8, 128), 1)
    own = lax.broadcasted_iota(jnp.int32, (16, 512), 1) % 16

    @pl.loop(0, steps)
    def _(step):
        first = step * per_step
        live = counts_ref[0] - first
        load(step).wait()

        def product(g, dst):
            left = []
            for q in range(16):
                s = g * 16 + q
                r = jnp.where(s < live, row_ref[first + s], 0)
                left.append(jnp.where(own == q, table[r], jnp.zeros((16, 512), BF16)))
            rows = pl.ds(pl.multiple_of(first + g * 16, 16), 16)
            right = jnp.concatenate([blocks[rows, t * 128 : (t + 1) * 128] for t in range(32)], 0)
            dst[...] = jnp.dot(jnp.concatenate(left, 0), right, **HIGH)

        def collect(g, src):
            for q in range(16):
                s = g * 16 + q
                c = jnp.where(s < live, col_ref[first + s], 2 * pairs)
                v = jnp.where(lane < 64, src[q * 16 : q * 16 + 8], src[q * 16 + 8 : q * 16 + 16])
                v = v + pltpu.roll(v, 64, 1)
                totals[c // 2] += jnp.where(lane // 64 == c % 2, v, 0.0)

        @pl.when(live > 0)
        def _():
            n = per_step // 16
            kept = (even, odd)
            product(0, even)
            for g in range(1, n):
                product(g, kept[g % 2])
                collect(g - 1, kept[(g - 1) % 2])
            collect(n - 1, kept[(n - 1) % 2])

    per = pairs // n_dest
    half = per // 2

    def store(e):
        return pltpu.make_async_copy(packed.at[e], out_hbm.at[e], out_sem.at[e])

    @pl.loop(0, n_dest)
    def _(e):
        @pl.loop(0, half // 16)
        def _(k):
            for u in range(16):
                at = k * 16 + u
                both = jnp.concatenate([totals[e * per + at], totals[e * per + half + at]], 0)
                packed[e, :, pl.ds(pl.multiple_of(at * 128, 128), 128)] = both.astype(BF16)

        store(e).start()

    @pl.loop(0, n_dest)
    def _(e):
        store(e).wait()


def spread_slots(counts, row_index, col_index, neigh, blocks, n_dest, slab_nodes):
    slots = blocks.shape[0]
    per_step = 128
    pairs = n_dest * slab_nodes // 128
    smem = pl.BlockSpec(memory_space=pltpu.SMEM)
    hbm = pl.BlockSpec(memory_space=pl.ANY)
    return pl.pallas_call(
        functools.partial(spread_kernel, per_step),
        in_specs=[smem, smem, smem, hbm, hbm],
        out_specs=hbm,
        out_shape=jax.ShapeDtypeStruct((n_dest, 16, slab_nodes // 2), BF16),
        scratch_shapes=[
            pltpu.VMEM(neigh.shape, BF16),
            pltpu.VMEM(blocks.shape, BF16),
            pltpu.VMEM((slab_nodes // 64, 16, 512), BF16),
            pltpu.VMEM((pairs + 1, 8, 128), F32),
            pltpu.VMEM((256, 128), F32),
            pltpu.VMEM((256, 128), F32),
            pltpu.VMEM((n_dest, 16, slab_nodes // 2), BF16),
            pltpu.SemaphoreType.DMA,
            pltpu.SemaphoreType.DMA((slots // per_step,)),
            pltpu.SemaphoreType.DMA((n_dest,)),
        ],
        compiler_params=pltpu.CompilerParams(vmem_limit_bytes=56 * MIB),
        name="spread_slots",
    )(counts, row_index, col_index, neigh, blocks)


def finish_kernel(
    n_feat, factor, grad_ref, pre_ref, w_ref, feat_ref, agg_ref, totals_hbm,
    out_ref, grad_self_ref, grad_neigh_ref,
    masked, back_send, back_recv, node_send, node_recv, terms, terms_recv, term, edge_recv,
    own, mine, one_recv, two_recv, three_send, three_recv, y_send, y_recv,
    back_ss, back_rs, node_ss, node_rs, term_ss, term_rs, edge_ss, edge_rs,
    load_sem, one_ss, one_rs, two_ss, two_rs, three_ss, three_rs, y_ss, y_rs,
):
    f = lax.axis_index("feat")
    e = lax.axis_index("edge")
    x, y = e // 2, e % 2
    n_edge = 8
    barrier = pltpu.get_barrier_semaphore()
    for k in range(1, n_feat):
        peer = {"feat": lax.rem(f + k, n_feat)}
        pl.semaphore_signal(barrier, inc=1, device_id=peer, device_id_type=MESH)
    for k in range(1, n_edge):
        peer = {"edge": lax.rem(e + k, n_edge)}
        pl.semaphore_signal(barrier, inc=1, device_id=peer, device_id_type=MESH)

    lanes = totals_hbm.shape[2] // 4

    def sub(j):
        return pl.ds(j * lanes, lanes)

    def edge_at(dx, py):
        return lax.rem(x + dx + 4, 4) * 2 + py

    def y_of(phase):
        return 1 - y if phase == 0 else y

    step_of = (1, -1)
    loads = []
    for phase in range(2):
        loads.append(
            pltpu.make_async_copy(totals_hbm.at[edge_at(0, y_of(phase))], own.at[phase], load_sem.at[3 * phase])
        )
        for d in range(2):
            loads.append(
                pltpu.make_async_copy(
                    totals_hbm.at[edge_at(step_of[d], y_of(phase)), :, pl.ds(d * 2 * lanes, 2 * lanes)],
                    mine.at[phase, d],
                    load_sem.at[3 * phase + 1 + d],
                )
            )
    for c in loads:
        c.start()

    def edge_copy(src, dst, send_sem, recv_sem, d):
        return pltpu.make_async_remote_copy(
            src_ref=src, dst_ref=dst, send_sem=send_sem, recv_sem=recv_sem,
            device_id={"edge": edge_at(step_of[d], y)}, device_id_type=MESH,
        )

    def one(p, d, j):
        src = totals_hbm.at[edge_at(2, y_of(p)), :, sub(2 * d + j)]
        return edge_copy(src, one_recv.at[p, d, j], one_ss.at[p, d, j], one_rs.at[p, d, j], d)

    def two(p, d, j):
        src = totals_hbm.at[edge_at(step_of[d], y_of(p)), :, sub(2 * (1 - d) + j)]
        return edge_copy(src, two_recv.at[p, d, j], two_ss.at[p, d, j], two_rs.at[p, d, j], d)

    def three(p, d, j):
        return edge_copy(
            three_send.at[p, d, j], three_recv.at[p, d, j], three_ss.at[p, d, j], three_rs.at[p, d, j], d
        )

    def y_copy(j):
        return pltpu.make_async_remote_copy(
            src_ref=y_send.at[j], dst_ref=y_recv.at[j], send_sem=y_ss.at[j], recv_sem=y_rs.at[j],
            device_id={"edge": edge_at(0, 1 - y)}, device_id_type=MESH,
        )

    def feat_copy(src, dst, send_sem, recv_sem, peer, slot):
        return pltpu.make_async_remote_copy(
            src_ref=src.at[peer], dst_ref=dst.at[slot], send_sem=send_sem.at[peer], recv_sem=recv_sem.at[slot],
            device_id={"feat": peer}, device_id_type=MESH,
        )

    def back_copy(peer, slot):
        return feat_copy(back_send, back_recv, back_ss, back_rs, peer, slot)

    def node_copy(peer, slot):
        return feat_copy(node_send, node_recv, node_ss, node_rs, peer, slot)

    def term_copy(peer, slot):
        return feat_copy(terms, terms_recv, term_ss, term_rs, peer, slot)

    def edge_term(peer, slot):
        return pltpu.make_async_remote_copy(
            src_ref=term, dst_ref=edge_recv.at[slot], send_sem=edge_ss.at[peer], recv_sem=edge_rs.at[slot],
            device_id={"edge": peer}, device_id_type=MESH,
        )

    def feat_peers():
        return [lax.rem(f + k, n_feat) for k in range(1, n_feat)]

    def edge_peers():
        return [lax.rem(e + k, n_edge) for k in range(1, n_edge)]

    pl.semaphore_wait(barrier, n_feat - 1 + n_edge - 1)
    for j in range(2):
        for d in range(2):
            one(0, d, j).start()
    for j in range(2):
        for d in range(2):
            two(0, d, j).start()

    nodes = grad_ref.shape[0]

    for owner in range(n_feat):
        span = slice(owner * nodes, (owner + 1) * nodes)
        both = jnp.concatenate([feat_ref[:, span].astype(F32), agg_ref[:, span].astype(F32)], 0)
        node_send[owner] = both.astype(BF16)
    for peer in feat_peers():
        node_copy(peer, f).start()
    masked[...] = masked_rows(grad_ref, pre_ref)
    product = lax.dot_general(w_ref[...], masked[...], NT, **HIGH)
    for owner in range(n_feat):
        halves_of(product, owner, back_send)
    for peer in feat_peers():
        back_copy(peer, f).start()
    node_recv[f] = node_send[f]
    back_recv[f] = back_send[f]
    for c in loads:
        c.wait()

    def relay(p):
        for j in range(2):
            for d in range(2):
                one(p, d, j).wait_recv()
                at = slice(j * lanes, (j + 1) * lanes)
                total = mine[p, d, :, at].astype(F32) + one_recv[p, d, j].astype(F32)
                three_send[p, d, j] = total.astype(BF16)
                three(p, d, j).start()

    def arrived(p, half, j):
        at = slice((2 * half + j) * lanes, (2 * half + j + 1) * lanes)
        return (
            own[p, :, at].astype(F32)
            + three_recv[p, half, j].astype(F32)
            + two_recv[p, 1 - half, j].astype(F32)
        )

    relay(0)
    for j in range(2):
        for d in range(2):
            one(1, d, j).start()
    for j in range(2):
        for d in range(2):
            two(1, d, j).start()

    for peer in feat_peers():
        node_copy(peer, peer).wait_recv()
    stacked = node_recv[...].reshape(n_feat * 16, nodes)
    partial = jnp.dot(stacked, masked[...], **HIGH)
    terms[...] = partial.reshape(terms.shape)
    for peer in feat_peers():
        term_copy(peer, f).start()

    for j in range(2):
        for half in range(2):
            two(0, 1 - half, j).wait_recv()
            three(0, half, j).wait_recv()
            y_send[2 * half + j] = arrived(0, half, j).astype(BF16)
            y_copy(2 * half + j).start()

    terms_recv[f] = terms[f]
    for peer in feat_peers():
        term_copy(peer, peer).wait_recv()
    total = terms_recv[0]
    for k in range(1, n_feat):
        total = total + terms_recv[k]
    term[...] = total
    for peer in edge_peers():
        edge_term(peer, e).start()

    relay(1)

    edge_recv[e] = term[...]
    for peer in edge_peers():
        edge_term(peer, peer).wait_recv()
    total = edge_recv[0]
    for k in range(1, n_edge):
        total = total + edge_recv[k]
    total = total * factor
    grad_self_ref[...] = total[:8]
    grad_neigh_ref[...] = total[8:]

    for peer in feat_peers():
        back_copy(peer, peer).wait_recv()
    half_lanes = 4 * lanes
    span = nodes // 2
    for j in range(2):
        for half in range(2):
            at = 2 * half + j
            two(1, 1 - half, j).wait_recv()
            three(1, half, j).wait_recv()
            y_copy(at).wait_recv()
            total = arrived(1, half, j) + y_recv[at].astype(F32)
            for h in range(2):
                for k in range(lanes // span):
                    low = at * lanes + k * span
                    node = h * half_lanes + low
                    src, part = node // nodes, node % nodes // span
                    back = back_recv[src].astype(F32)[part * 8 : part * 8 + 8]
                    out_ref[:, node : node + span] = (
                        total[h * 8 : h * 8 + 8, k * span : (k + 1) * span] + back
                    ).astype(BF16)

    for p in range(2):
        for j in range(2):
            for d in range(2):
                one(p, d, j).wait_send()
                two(p, d, j).wait_send()
                three(p, d, j).wait_send()
    for j in range(4):
        y_copy(j).wait_send()
    for peer in feat_peers():
        node_copy(peer, f).wait_send()
        back_copy(peer, f).wait_send()
        term_copy(peer, f).wait_send()
    for peer in edge_peers():
        edge_term(peer, e).wait_send()


def finish(grad_out, pre_act, w_self, feat_t, agg_t, totals, n_feat, factor):
    nodes, hidden = grad_out.shape
    n_edge, _, half = totals.shape
    features, slab = feat_t.shape
    lanes = half // 4
    vmem = pl.BlockSpec(memory_space=pltpu.VMEM)
    dma = pltpu.SemaphoreType.DMA
    return pl.pallas_call(
        functools.partial(finish_kernel, n_feat, factor),
        in_specs=[vmem] * 5 + [pl.BlockSpec(memory_space=pl.ANY)],
        out_specs=[vmem] * 3,
        out_shape=[
            jax.ShapeDtypeStruct((features, slab), BF16),
            jax.ShapeDtypeStruct((features, hidden), F32),
            jax.ShapeDtypeStruct((features, hidden), F32),
        ],
        scratch_shapes=[
            pltpu.VMEM((nodes, hidden), BF16),
            pltpu.VMEM((n_feat, 16, nodes // 2), BF16),
            pltpu.VMEM((n_feat, 16, nodes // 2), BF16),
            pltpu.VMEM((n_feat, 16, nodes), BF16),
            pltpu.VMEM((n_feat, 16, nodes), BF16),
            pltpu.VMEM((n_feat, 16, hidden), F32),
            pltpu.VMEM((n_feat, 16, hidden), F32),
            pltpu.VMEM((16, hidden), F32),
            pltpu.VMEM((n_edge, 16, hidden), F32),
            pltpu.VMEM((2, 16, half), BF16),
            pltpu.VMEM((2, 2, 16, 2 * lanes), BF16),
            pltpu.VMEM((2, 2, 2, 16, lanes), BF16),
            pltpu.VMEM((2, 2, 2, 16, lanes), BF16),
            pltpu.VMEM((2, 2, 2, 16, lanes), BF16),
            pltpu.VMEM((2, 2, 2, 16, lanes), BF16),
            pltpu.VMEM((4, 16, lanes), BF16),
            pltpu.VMEM((4, 16, lanes), BF16),
            dma((n_feat,)), dma((n_feat,)), dma((n_feat,)), dma((n_feat,)),
            dma((n_feat,)), dma((n_feat,)), dma((n_edge,)), dma((n_edge,)),
            dma((6,)), dma((2, 2, 2)), dma((2, 2, 2)), dma((2, 2, 2)), dma((2, 2, 2)),
            dma((2, 2, 2)), dma((2, 2, 2)), dma((4,)), dma((4,)),
        ],
        compiler_params=pltpu.CompilerParams(
            collective_id=1, has_side_effects=True, vmem_limit_bytes=48 * MIB
        ),
        name="finish",
    )(grad_out, pre_act, w_self, feat_t, agg_t, totals)


def on_device(grad_out, pre_act, feat_t, agg_t, w_self, w_neigh, blocks, row_index, col_index, counts):
    n_feat = lax.axis_size("feat")
    n_edge = lax.axis_size("edge")
    slab_nodes = feat_t.shape[1]
    factor = 1.0 / math.sqrt(slab_nodes * n_edge)
    neigh = send_neigh(grad_out, pre_act, w_neigh, n_feat)
    totals = spread_slots(counts, row_index, col_index, neigh, blocks, n_edge, slab_nodes)
    grad_feat_t, grad_w_self, grad_w_neigh = finish(
        grad_out, pre_act, w_self, feat_t, agg_t, totals, n_feat, factor
    )
    return (grad_feat_t, grad_w_self, grad_w_neigh)


def solution(mesh):
    in_specs = (
        P(("edge", "feat"), None),
        P(("edge", "feat"), None),
        P("feat", "edge"),
        P("feat", "edge"),
        P(),
        P(),
        P("edge", None),
        P("edge"),
        P("edge"),
        P("edge"),
    )
    out_specs = (P("feat", "edge"), P("feat", None), P("feat", None))
    return jax.shard_map(
        on_device, mesh=mesh, in_specs=in_specs, out_specs=out_specs, check_vma=False
    )
```

```python
import functools
import math

import jax
import jax.numpy as jnp
from jax import lax
from jax.experimental import pallas as pl
from jax.experimental.pallas import tpu as pltpu
from jax.sharding import PartitionSpec as P

MESH = pl.DeviceIdType.MESH
MIB = 2**20
F32 = jnp.float32
BF16 = jnp.bfloat16
HIGH = dict(preferred_element_type=F32)
NT = (((1,), (1,)), ((), ()))


def masked_rows(grad_ref, pre_ref):
    return jnp.where(pre_ref[...] > 0, grad_ref[...], jnp.zeros_like(grad_ref))


def halves_of(product, owner):
    nodes = product.shape[1]
    rows = product[owner * 8 : owner * 8 + 8]
    both = jnp.concatenate([rows[:, : nodes // 2], rows[:, nodes // 2 :]], 0)
    return both.astype(BF16)


def find_chains(count_ref, col_smem, row_ref, col_ref, row_out, prev_out, last_out):
    slots = row_ref.shape[0] * 128
    count = count_ref[0]

    def count_up(shape):
        return lax.broadcasted_iota(jnp.int32, shape, 0) * 128 + lax.broadcasted_iota(jnp.int32, shape, 1)

    spot = count_up(row_ref.shape)
    alive = spot < count
    row_out[...] = jnp.where(alive, row_ref[...], 0)
    cols = jnp.where(alive, col_ref[...], -2)
    names = count_up(last_out.shape)

    def body(i, carry):
        prev, last = carry
        for u in range(32):
            s = i * 32 + u
            c = jnp.where(s < count, col_smem[s], -1)
            prev = jnp.where((cols == c) & (spot > s), s, prev)
            last = jnp.where(names == c, s, last)
        return prev, last

    none = (jnp.full(row_ref.shape, slots, jnp.int32), jnp.full(last_out.shape, slots, jnp.int32))
    prev, last = lax.fori_loop(0, slots // 32, body, none)
    prev_out[...] = prev
    last_out[...] = last


def build_table(src, neigh, table, permute_ref):
    tiles = neigh.shape[2] // 128
    x = jnp.concatenate([neigh[src, :, t * 128 : (t + 1) * 128] for t in range(tiles)], 0)
    for b in range(2):
        y = jnp.dot(x, permute_ref[:, b * 512 : (b + 1) * 512], **HIGH)
        for t in range(tiles):
            for h in range(2):
                at = t * 16 + h * 8
                both = jnp.concatenate([y[at : at + 8, :256], y[at : at + 8, 256:]], 0)
                table[src * (4 * tiles) + h * 2 * tiles + 2 * t + b] = both.astype(BF16)


def permutation():
    place = lax.broadcasted_iota(jnp.int32, (128, 1024), 1)
    source = place // 512 * 64 + (place % 256) // 8 * 2 + place // 256 % 2
    node = lax.broadcasted_iota(jnp.int32, (128, 1024), 0)
    return jnp.where(source == node, 1.0, 0.0).astype(BF16)


def products(row_smem, prev_smem, blocks, table, sums, even, odd):
    slots = blocks.shape[0]
    steps = slots // 128
    lane = lax.broadcasted_iota(jnp.int32, (8, 128), 1)
    own = lax.broadcasted_iota(jnp.int32, (16, 256), 1) % 8
    sums[slots] = jnp.zeros((8, 128), F32)

    def product(step, g, dst):
        rows = pl.ds(pl.multiple_of(step * 128 + g * 16, 16), 16)
        tiles = [blocks[rows, t * 128 : (t + 1) * 128].astype(F32) for t in range(32)]
        for h in range(2):
            left = []
            for q in range(8):
                mine = table[row_smem[step, g * 16 + h * 8 + q]]
                left.append(jnp.where(own == q, mine, jnp.zeros((16, 256), BF16)))
            right = jnp.concatenate([t[h * 8 : h * 8 + 8] for t in tiles], 0).astype(BF16)
            dst[h * 128 : h * 128 + 128] = jnp.dot(jnp.concatenate(left, 0), right, **HIGH)

    def collect(step, g, src):
        for q in range(16):
            before = sums[prev_smem[step, g * 16 + q]]
            v = jnp.where(lane < 64, src[q * 16 : q * 16 + 8], src[q * 16 + 8 : q * 16 + 16])
            sums[step * 128 + g * 16 + q] = v + before

    kept = (even, odd)
    product(0, 0, even)

    @pl.loop(0, steps)
    def _(step):
        for g in range(8):
            if g < 7:
                product(step, g + 1, kept[(g + 1) % 2])
            else:
                product(jnp.minimum(step + 1, steps - 1), 0, even)
            collect(step, g, kept[g % 2])


def pack(e, last_smem, sums, out_ref):
    half = out_ref.shape[1]
    rows = half // 64 // 128
    lane = lax.broadcasted_iota(jnp.int32, (8, 128), 1)
    for k in range(rows):

        @pl.loop(0, 4)
        def _(v):
            low = pl.multiple_of(k * 8192 + v * 2048, 2048)
            tiles = []
            for u in range(16):
                two = []
                for h in range(2):
                    r = (e * 2 + h) * rows + k
                    a = sums[last_smem[r, v * 32 + 2 * u]]
                    b = sums[last_smem[r, v * 32 + 2 * u + 1]]
                    two.append(jnp.where(lane < 64, a, b) + pltpu.roll(jnp.where(lane < 64, b, a), 64, 1))
                tiles.append(jnp.concatenate(two, 0).astype(BF16))
            out_ref[:, pl.ds(low, 2048)] = jnp.concatenate(tiles, 1)


X_FIRST = 5120
SUBS = ((0, 2048), (2048, 5120))


def layer_kernel(
    n_feat, factor, count_ref, col_smem, index_ref, w_self_ref, w_neigh_ref, grad_hbm, pre_hbm, feat_hbm, agg_hbm,
    blocks_hbm, out_ref, weight_ref,
    grad, pre, feat, agg, blocks, masked, permute, table, sums, even, odd, packed,
    row_v, prev_v, last_v, row_s, prev_s, last_s,
    neigh_send, neigh, back_send, back_recv, node_send, node_recv, terms, terms_recv, term, edge_recv,
    one_recv, two_recv, three_send, three_recv, y_send, y_recv,
    yf_recv, t_sum, t_one, t_two, t_three_send, t_three_recv,
    load_sem, index_sem, neigh_ss, neigh_rs, back_ss, back_rs, node_ss, node_rs, term_ss, term_rs, edge_ss, edge_rs,
    one_ss, one_rs, two_ss, two_rs, three_ss, three_rs, y_ss, y_rs,
    yf_ss, yf_rs, t_one_ss, t_one_rs, t_two_ss, t_two_rs, t_three_ss, t_three_rs,
):
    f = lax.axis_index("feat")
    e = lax.axis_index("edge")
    x, y = e // 2, e % 2
    n_edge = 8
    barrier = pltpu.get_barrier_semaphore()

    @pl.loop(1, n_feat)
    def _(k):
        peer = {"feat": lax.rem(f + k, n_feat)}
        pl.semaphore_signal(barrier, inc=1, device_id=peer, device_id_type=MESH)

    @pl.loop(1, n_edge)
    def _(k):
        peer = {"edge": lax.rem(e + k, n_edge)}
        pl.semaphore_signal(barrier, inc=1, device_id=peer, device_id_type=MESH)

    pairs = ((grad_hbm, grad), (pre_hbm, pre), (feat_hbm, feat), (agg_hbm, agg), (blocks_hbm, blocks))
    loads = [pltpu.make_async_copy(a, b, load_sem.at[i]) for i, (a, b) in enumerate(pairs)]
    for c in loads:
        c.start()

    def to_feat(src, dst, send_sem, recv_sem):
        def copy(peer, slot):
            return pltpu.make_async_remote_copy(
                src_ref=src.at[peer], dst_ref=dst.at[slot], send_sem=send_sem.at[peer], recv_sem=recv_sem.at[slot],
                device_id={"feat": peer}, device_id_type=MESH,
            )

        return copy

    neigh_copy = to_feat(neigh_send, neigh, neigh_ss, neigh_rs)
    back_copy = to_feat(back_send, back_recv, back_ss, back_rs)
    node_copy = to_feat(node_send, node_recv, node_ss, node_rs)
    term_copy = to_feat(terms, terms_recv, term_ss, term_rs)

    def start_all(copy):
        @pl.loop(1, n_feat)
        def _(k):
            copy(lax.rem(f + k, n_feat), f).start()

    def receive_all(copy):
        @pl.loop(1, n_feat)
        def _(k):
            peer = lax.rem(f + k, n_feat)
            copy(peer, peer).wait_recv()

    def sent_all(copy):
        @pl.loop(1, n_feat)
        def _(k):
            copy(lax.rem(f + k, n_feat), f).wait_send()

    loads[0].wait()
    loads[1].wait()
    masked[...] = masked_rows(grad, pre)
    nodes = grad.shape[0]
    product = lax.dot_general(w_neigh_ref[...], masked[...], NT, **HIGH)
    for owner in range(n_feat):
        neigh_send[owner] = halves_of(product, owner)
    pl.semaphore_wait(barrier, n_feat - 1 + n_edge - 1)
    start_all(neigh_copy)

    neigh[f] = neigh_send[f]
    permute[...] = permutation()
    find_chains(count_ref, col_smem, index_ref.at[0], index_ref.at[1], row_v, prev_v, last_v)
    places = ((row_v, row_s), (prev_v, prev_s), (last_v, last_s))
    moves = [pltpu.make_async_copy(a, b, index_sem.at[i]) for i, (a, b) in enumerate(places)]
    for c in moves:
        c.start()
    product = lax.dot_general(w_self_ref[...], masked[...], NT, **HIGH)
    for owner in range(n_feat):
        back_send[owner] = halves_of(product, owner)
    loads[2].wait()
    loads[3].wait()
    for owner in range(n_feat):
        span = slice(owner * nodes, (owner + 1) * nodes)
        both = jnp.concatenate([feat[:, span].astype(F32), agg[:, span].astype(F32)], 0)
        node_send[owner] = both.astype(BF16)
    node_recv[f] = node_send[f]
    back_recv[f] = back_send[f]
    build_table(f, neigh, table, permute)

    @pl.loop(1, n_feat)
    def _(k):
        peer = lax.rem(f + k, n_feat)
        neigh_copy(peer, peer).wait_recv()
        build_table(peer, neigh, table, permute)

    start_all(node_copy)
    start_all(back_copy)
    for c in moves:
        c.wait()
    loads[4].wait()
    products(row_s, prev_s, blocks, table, sums, even, odd)

    half = packed.shape[3] // 2
    step_of = (1, -1)
    OPP, RIGHT, LEFT, OWN = range(4)
    away = {OPP: 2, RIGHT: 1, LEFT: -1, OWN: 0}

    def edge_at(dx, py):
        return lax.rem(x + dx + 4, 4) * 2 + py

    def along_x(src, dst, send_sem, recv_sem, d):
        return pltpu.make_async_remote_copy(
            src_ref=src, dst_ref=dst, send_sem=send_sem, recv_sem=recv_sem,
            device_id={"edge": edge_at(step_of[d], y)}, device_id_type=MESH,
        )

    def along_y(src, dst, send_sem, recv_sem):
        return pltpu.make_async_remote_copy(
            src_ref=src, dst_ref=dst, send_sem=send_sem, recv_sem=recv_sem,
            device_id={"edge": edge_at(0, 1 - y)}, device_id_type=MESH,
        )

    def lanes_of(h, low, high):
        return pl.ds(h * half + low, high - low)

    def sub(j):
        return pl.ds(SUBS[j][0], SUBS[j][1] - SUBS[j][0])

    def one(p, d, j):
        src = packed.at[p, OPP, :, lanes_of(d, *SUBS[j])]
        return along_x(src, one_recv.at[p, d, :, sub(j)], one_ss.at[p, d, j], one_rs.at[p, d, j], d)

    def two(p, d, j):
        src = packed.at[p, RIGHT + d, :, lanes_of(1 - d, *SUBS[j])]
        return along_x(src, two_recv.at[p, d, :, sub(j)], two_ss.at[p, d, j], two_rs.at[p, d, j], d)

    def three(p, d, j):
        return along_x(
            three_send.at[p, d, :, sub(j)], three_recv.at[p, d, :, sub(j)],
            three_ss.at[p, d, j], three_rs.at[p, d, j], d,
        )

    def y_copy(h, j):
        return along_y(y_send.at[h, :, sub(j)], y_recv.at[h, :, sub(j)], y_ss.at[h, j], y_rs.at[h, j])

    def yf_copy(i, h):
        src = packed.at[0, i, :, lanes_of(h, X_FIRST, half)]
        return along_y(src, yf_recv.at[i, h], yf_ss.at[i, h], yf_rs.at[i, h])

    def t_one_copy(d):
        return along_x(t_sum.at[OPP, d], t_one.at[d], t_one_ss.at[d], t_one_rs.at[d], d)

    def t_two_copy(d):
        return along_x(t_sum.at[RIGHT + d, 1 - d], t_two.at[d], t_two_ss.at[d], t_two_rs.at[d], d)

    def t_three_copy(d):
        return along_x(t_three_send.at[d], t_three_recv.at[d], t_three_ss.at[d], t_three_rs.at[d], d)

    both_ways = [(j, d) for j in range(2) for d in range(2)]

    def pack_to(p, i):
        pack(edge_at(away[i], 1 - y if p == 0 else y), last_s, sums, packed.at[p, i])

    pack_to(0, OPP)
    for j, d in both_ways:
        one(0, d, j).start()
    for h in range(2):
        yf_copy(OPP, h).start()
    for d in range(2):
        pack_to(0, RIGHT + d)
        for j in range(2):
            two(0, d, j).start()
        for h in range(2):
            yf_copy(RIGHT + d, h).start()
    pack_to(0, OWN)
    for h in range(2):
        yf_copy(OWN, h).start()
    pack_to(1, OPP)

    def relay(p):
        for j, d in both_ways:
            one(p, d, j).wait_recv()
            low, high = SUBS[j]
            mine = packed[p, RIGHT + d, :, d * half + low : d * half + high].astype(F32)
            three_send[p, d, :, low:high] = (mine + one_recv[p, d, :, low:high].astype(F32)).astype(BF16)
            three(p, d, j).start()

    relay(0)
    for j, d in both_ways:
        one(1, d, j).start()
    for d in range(2):
        pack_to(1, RIGHT + d)
        for j in range(2):
            two(1, d, j).start()
    pack_to(1, OWN)

    receive_all(node_copy)
    stacked = node_recv[...].reshape(n_feat * 16, nodes)
    terms[...] = jnp.dot(stacked, masked[...], **HIGH).reshape(terms.shape)
    start_all(term_copy)
    terms_recv[f] = terms[f]

    def sum_y(i):
        for h in range(2):
            yf_copy(i, h).wait_recv()
            mine = packed[1, i, :, h * half + X_FIRST : (h + 1) * half].astype(F32)
            t_sum[i, h] = (mine + yf_recv[i, h].astype(F32)).astype(BF16)

    sum_y(OPP)
    for d in range(2):
        t_one_copy(d).start()
    for d in range(2):
        sum_y(RIGHT + d)
        t_two_copy(d).start()
    sum_y(OWN)

    def arrived(p, h, low, high):
        return (
            packed[p, OWN, :, h * half + low : h * half + high].astype(F32)
            + three_recv[p, h, :, low:high].astype(F32)
            + two_recv[p, 1 - h, :, low:high].astype(F32)
        )

    for j, h in both_ways:
        two(0, 1 - h, j).wait_recv()
        three(0, h, j).wait_recv()
        y_send[h, :, SUBS[j][0] : SUBS[j][1]] = arrived(0, h, *SUBS[j]).astype(BF16)
        y_copy(h, j).start()

    relay(1)
    for d in range(2):
        t_one_copy(d).wait_recv()
        t_three_send[d] = (t_sum[RIGHT + d, d].astype(F32) + t_one[d].astype(F32)).astype(BF16)
        t_three_copy(d).start()

    receive_all(term_copy)
    total = terms_recv[0]
    for k in range(1, n_feat):
        total = total + terms_recv[k]
    term[...] = total

    def edge_term(peer, slot):
        return pltpu.make_async_remote_copy(
            src_ref=term, dst_ref=edge_recv.at[slot], send_sem=edge_ss.at[peer], recv_sem=edge_rs.at[slot],
            device_id={"edge": peer}, device_id_type=MESH,
        )

    @pl.loop(1, n_edge)
    def _(k):
        edge_term(lax.rem(e + k, n_edge), e).start()

    edge_recv[e] = term[...]
    receive_all(back_copy)

    def finish(h, low, total):
        span = nodes // 2
        for r in range(2):
            for k in range(total.shape[1] // span):
                node = r * 2 * half + h * half + low + k * span
                src, part = node // nodes, node % nodes // span
                back = back_recv[src].astype(F32)[part * 8 : part * 8 + 8]
                rows = total[r * 8 : r * 8 + 8, k * span : (k + 1) * span]
                out_ref[:, node : node + span] = (rows + back).astype(BF16)

    for j, h in both_ways:
        low, high = SUBS[j]
        two(1, 1 - h, j).wait_recv()
        three(1, h, j).wait_recv()
        y_copy(h, j).wait_recv()
        finish(h, low, arrived(1, h, low, high) + y_recv[h, :, low:high].astype(F32))
    for h in range(2):
        t_two_copy(1 - h).wait_recv()
        t_three_copy(h).wait_recv()
        finish(h, X_FIRST, t_sum[OWN, h].astype(F32) + t_three_recv[h].astype(F32) + t_two[1 - h].astype(F32))

    @pl.loop(1, n_edge)
    def _(k):
        peer = lax.rem(e + k, n_edge)
        edge_term(peer, peer).wait_recv()

    total = edge_recv[0]
    for k in range(1, n_edge):
        total = total + edge_recv[k]
    weight_ref[...] = total * factor

    for copy in (neigh_copy, back_copy, node_copy, term_copy):
        sent_all(copy)

    @pl.loop(1, n_edge)
    def _(k):
        edge_term(lax.rem(e + k, n_edge), e).wait_send()

    for p in range(2):
        for j, d in both_ways:
            one(p, d, j).wait_send()
            two(p, d, j).wait_send()
            three(p, d, j).wait_send()
    for j, h in both_ways:
        y_copy(h, j).wait_send()
    for i in range(4):
        for h in range(2):
            yf_copy(i, h).wait_send()
    for d in range(2):
        t_one_copy(d).wait_send()
        t_two_copy(d).wait_send()
        t_three_copy(d).wait_send()


def layer(counts, row_index, col_index, w_self, w_neigh, grad_out, pre_act, feat_t, agg_t, blocks, n_feat, n_edge, factor):
    nodes, hidden = grad_out.shape
    features, slab = feat_t.shape
    slots = blocks.shape[0]
    half = slab // 4
    y_first = half - X_FIRST
    names = n_edge * slab // 64
    index = jnp.stack([row_index, col_index]).reshape(2, slots // 128, 128)
    smem = pl.BlockSpec(memory_space=pltpu.SMEM)
    vmem = pl.BlockSpec(memory_space=pltpu.VMEM)
    hbm = pl.BlockSpec(memory_space=pl.ANY)
    dma = pltpu.SemaphoreType.DMA
    ints = [(slots // 128, 128), (slots // 128, 128), (names // 128, 128)]
    small, large = (n_feat, 16, nodes // 2), (n_feat, 16, nodes)
    x_part = (2, 2, 16, X_FIRST)
    y_part = (2, 16, X_FIRST)
    return pl.pallas_call(
        functools.partial(layer_kernel, n_feat, factor),
        in_specs=[smem, smem, vmem, vmem, vmem] + [hbm] * 5,
        out_specs=[vmem] * 2,
        out_shape=[
            jax.ShapeDtypeStruct((features, slab), BF16),
            jax.ShapeDtypeStruct((2 * features, hidden), F32),
        ],
        scratch_shapes=[
            pltpu.VMEM((nodes, hidden), BF16),
            pltpu.VMEM((nodes, hidden), BF16),
            pltpu.VMEM((features, slab), BF16),
            pltpu.VMEM((features, slab), BF16),
            pltpu.VMEM(blocks.shape, BF16),
            pltpu.VMEM((nodes, hidden), BF16),
            pltpu.VMEM((128, 1024), BF16),
            pltpu.VMEM((slab // 64, 16, 256), BF16),
            pltpu.VMEM((slots + 1, 8, 128), F32),
            pltpu.VMEM((256, 128), F32),
            pltpu.VMEM((256, 128), F32),
            pltpu.VMEM((2, 4, 16, 2 * half), BF16),
            *[pltpu.VMEM(i, jnp.int32) for i in ints],
            *[pltpu.SMEM(i, jnp.int32) for i in ints],
            *[pltpu.VMEM(i, BF16) for i in (small, small, small, small, large, large)],
            pltpu.VMEM((n_feat, 16, hidden), F32),
            pltpu.VMEM((n_feat, 16, hidden), F32),
            pltpu.VMEM((16, hidden), F32),
            pltpu.VMEM((n_edge, 16, hidden), F32),
            *[pltpu.VMEM(i, BF16) for i in (x_part, x_part, x_part, x_part, y_part, y_part)],
            *[pltpu.VMEM((4, 2, 16, y_first), BF16) for i in range(2)],
            *[pltpu.VMEM((2, 16, y_first), BF16) for i in range(4)],
            dma((5,)),
            dma((3,)),
            *[dma((n_feat,)) for i in range(8)],
            dma((n_edge,)),
            dma((n_edge,)),
            *[dma((2, 2, 2)) for i in range(6)],
            dma((2, 2)),
            dma((2, 2)),
            dma((4, 2)),
            dma((4, 2)),
            *[dma((2,)) for i in range(6)],
        ],
        compiler_params=pltpu.CompilerParams(collective_id=0, has_side_effects=True, vmem_limit_bytes=60 * MIB),
        name="layer",
    )(counts, col_index, index, w_self, w_neigh, grad_out, pre_act, feat_t, agg_t, blocks)


def on_device(grad_out, pre_act, feat_t, agg_t, w_self, w_neigh, blocks, row_index, col_index, counts):
    n_feat = lax.axis_size("feat")
    n_edge = lax.axis_size("edge")
    features, slab = feat_t.shape
    factor = 1.0 / math.sqrt(slab * n_edge)
    grad_feat_t, weights = layer(
        counts, row_index, col_index, w_self, w_neigh, grad_out, pre_act, feat_t, agg_t, blocks, n_feat, n_edge, factor
    )
    return (grad_feat_t, weights[:features], weights[features:])


def solution(mesh):
    in_specs = (
        P(("edge", "feat"), None),
        P(("edge", "feat"), None),
        P("feat", "edge"),
        P("feat", "edge"),
        P(),
        P(),
        P("edge", None),
        P("edge"),
        P("edge"),
        P("edge"),
    )
    out_specs = (P("feat", "edge"), P("feat", None), P("feat", None))
    return jax.shard_map(
        on_device, mesh=mesh, in_specs=in_specs, out_specs=out_specs, check_vma=False
    )
```

```python
import functools
import math

import jax
import jax.numpy as jnp
from jax import lax
from jax.experimental import pallas as pl
from jax.experimental.pallas import tpu as pltpu
from jax.sharding import PartitionSpec as P

MESH = pl.DeviceIdType.MESH
MIB = 2**20
F32 = jnp.float32
BF16 = jnp.bfloat16
HIGH = dict(preferred_element_type=F32)
NT = (((1,), (1,)), ((), ()))


def masked_rows(grad_ref, pre_ref):
    return jnp.where(pre_ref[...] > 0, grad_ref[...], jnp.zeros_like(grad_ref))


def halves_of(product, owner):
    nodes = product.shape[1]
    rows = product[owner * 8 : owner * 8 + 8]
    both = jnp.concatenate([rows[:, : nodes // 2], rows[:, nodes // 2 :]], 0)
    return both.astype(BF16)


def find_chains(count_ref, col_smem, row_ref, col_ref, row_out, prev_out, last_out):
    slots = row_ref.shape[0] * 128
    count = count_ref[0]

    def count_up(shape):
        return lax.broadcasted_iota(jnp.int32, shape, 0) * 128 + lax.broadcasted_iota(jnp.int32, shape, 1)

    spot = count_up(row_ref.shape)
    alive = spot < count
    row_out[...] = jnp.where(alive, row_ref[...], 0)
    cols = [jnp.where(alive & (spot % 2 == k), col_ref[...], -2) for k in range(2)]
    names = count_up(last_out.shape[1:])

    def body(i, carry):
        prev, last = carry[0], list(carry[1:])
        for u in range(32):
            s = i * 32 + u
            place = i * 16 + u // 2
            c = jnp.where(s < count, col_smem[s], -1)
            prev = jnp.where((cols[u % 2] == c) & (spot > s), place, prev)
            last[u % 2] = jnp.where(names == c, place, last[u % 2])
        return prev, *last

    none = [jnp.full(n, slots // 2, jnp.int32) for n in (row_ref.shape, names.shape, names.shape)]
    prev, *last = lax.fori_loop(0, slots // 32, body, tuple(none))
    prev_out[...] = prev
    for k in range(2):
        last_out[k] = last[k]


def build_table(sources, neigh, table, permute_ref):
    tiles = neigh.shape[2] // 128
    x = jnp.concatenate([neigh[i, :, t * 128 : (t + 1) * 128] for i in sources for t in range(tiles)], 0)
    for b in range(2):
        y = jnp.dot(x, permute_ref[:, b * 512 : (b + 1) * 512], **HIGH)
        for n, i in enumerate(sources):
            for t in range(tiles):
                for h in range(2):
                    at = (n * tiles + t) * 16 + h * 8
                    both = jnp.concatenate([y[at : at + 8, :256], y[at : at + 8, 256:]], 0)
                    table[i * (4 * tiles) + h * 2 * tiles + 2 * t + b] = both.astype(BF16)


def permutation():
    place = lax.broadcasted_iota(jnp.int32, (128, 1024), 1)
    source = place // 512 * 64 + (place % 256) // 8 * 2 + place // 256 % 2
    node = lax.broadcasted_iota(jnp.int32, (128, 1024), 0)
    return jnp.where(source == node, 1.0, 0.0).astype(BF16)


def products(row_smem, prev_smem, blocks, table, sums, even, odd):
    slots = blocks.shape[0]
    steps = slots // 128
    lane = lax.broadcasted_iota(jnp.int32, (8, 128), 1)
    own = lax.broadcasted_iota(jnp.int32, (16, 256), 1) % 8
    for k in range(2):
        sums[k][slots // 2] = jnp.zeros((8, 128), F32)

    def product(step, g, dst):
        rows = pl.ds(pl.multiple_of(step * 128 + g * 16, 16), 16)
        tiles = [blocks[rows, t * 128 : (t + 1) * 128].astype(F32) for t in range(32)]
        for h in range(2):
            left = []
            for q in range(8):
                mine = table[row_smem[step, g * 16 + h * 8 + q]]
                left.append(jnp.where(own == q, mine, jnp.zeros((16, 256), BF16)))
            right = jnp.concatenate([t[h * 8 : h * 8 + 8] for t in tiles], 0).astype(BF16)
            dst[h * 128 : h * 128 + 128] = jnp.dot(jnp.concatenate(left, 0), right, **HIGH)

    def collect(step, g, src):
        for q in range(16):
            before = sums[q % 2][prev_smem[step, g * 16 + q]]
            v = jnp.where(lane < 64, src[q * 16 : q * 16 + 8], src[q * 16 + 8 : q * 16 + 16])
            sums[q % 2][step * 64 + g * 8 + q // 2] = v + before

    kept = (even, odd)
    product(0, 0, even)

    @pl.loop(0, steps)
    def _(step):
        for g in range(8):
            if g < 7:
                product(step, g + 1, kept[(g + 1) % 2])
            else:
                product(jnp.minimum(step + 1, steps - 1), 0, even)
            collect(step, g, kept[g % 2])


def pack(e, last_smem, sums, out_ref):
    half = out_ref.shape[1]
    rows = half // 64 // 128
    lane = lax.broadcasted_iota(jnp.int32, (8, 128), 1)
    for k in range(rows):

        @pl.loop(0, 4)
        def _(v):
            low = pl.multiple_of(k * 8192 + v * 2048, 2048)
            tiles = []
            for u in range(16):
                two = []
                for h in range(2):
                    r = (e * 2 + h) * rows + k
                    a, b = [
                        sums[0][last_smem[0, r, v * 32 + 2 * u + w]] + sums[1][last_smem[1, r, v * 32 + 2 * u + w]]
                        for w in range(2)
                    ]
                    two.append(jnp.where(lane < 64, a, b) + pltpu.roll(jnp.where(lane < 64, b, a), 64, 1))
                tiles.append(jnp.concatenate(two, 0).astype(BF16))
            out_ref[:, pl.ds(low, 2048)] = jnp.concatenate(tiles, 1)


X_FIRST = 5120
SUBS = ((0, 2048), (2048, 5120))


def layer_kernel(
    n_feat, factor, count_ref, col_smem, row_hbm, col_hbm, w_self_hbm, w_neigh_hbm, grad_hbm, pre_hbm, feat_hbm, agg_hbm,
    blocks_hbm, out_ref, weight_ref,
    w_neigh, grad, pre, row, col, w_self, feat, agg, blocks, masked, permute, table, sums_even, sums_odd, even, odd, packed,
    row_v, prev_v, last_v, row_s, prev_s, last_s,
    neigh_send, neigh, back_send, back_recv, node_send, node_recv, terms, terms_recv, term, edge_recv,
    one_recv, two_recv, three_send, three_recv, y_send, y_recv,
    yf_recv, t_sum, t_one, t_two, t_three_send, t_three_recv,
    load_sem, index_sem, neigh_ss, neigh_rs, back_ss, back_rs, node_ss, node_rs, term_ss, term_rs, edge_ss, edge_rs,
    one_ss, one_rs, two_ss, two_rs, three_ss, three_rs, y_ss, y_rs,
    yf_ss, yf_rs, t_one_ss, t_one_rs, t_two_ss, t_two_rs, t_three_ss, t_three_rs,
):
    f = lax.axis_index("feat")
    e = lax.axis_index("edge")
    x, y = e // 2, e % 2
    n_edge = 8
    sums = (sums_even, sums_odd)
    barrier = pltpu.get_barrier_semaphore()

    @pl.loop(1, n_feat)
    def _(k):
        peer = {"feat": lax.rem(f + k, n_feat)}
        pl.semaphore_signal(barrier, inc=1, device_id=peer, device_id_type=MESH)

    @pl.loop(1, n_edge)
    def _(k):
        peer = {"edge": lax.rem(e + k, n_edge)}
        pl.semaphore_signal(barrier, inc=1, device_id=peer, device_id_type=MESH)

    pairs = (
        (w_neigh_hbm, w_neigh), (grad_hbm, grad), (pre_hbm, pre), (row_hbm, row), (col_hbm, col),
        (w_self_hbm, w_self), (feat_hbm, feat), (agg_hbm, agg), (blocks_hbm, blocks),
    )
    loads = [pltpu.make_async_copy(a, b, load_sem.at[i]) for i, (a, b) in enumerate(pairs)]
    for c in loads[:3]:
        c.start()

    def to_feat(src, dst, send_sem, recv_sem):
        def copy(peer, slot):
            return pltpu.make_async_remote_copy(
                src_ref=src.at[peer], dst_ref=dst.at[slot], send_sem=send_sem.at[peer], recv_sem=recv_sem.at[slot],
                device_id={"feat": peer}, device_id_type=MESH,
            )

        return copy

    neigh_copy = to_feat(neigh_send, neigh, neigh_ss, neigh_rs)
    back_copy = to_feat(back_send, back_recv, back_ss, back_rs)
    node_copy = to_feat(node_send, node_recv, node_ss, node_rs)
    term_copy = to_feat(terms, terms_recv, term_ss, term_rs)

    def start_all(copy):
        @pl.loop(1, n_feat)
        def _(k):
            copy(lax.rem(f + k, n_feat), f).start()

    def receive_all(copy):
        @pl.loop(1, n_feat)
        def _(k):
            peer = lax.rem(f + k, n_feat)
            copy(peer, peer).wait_recv()

    def sent_all(copy):
        @pl.loop(1, n_feat)
        def _(k):
            copy(lax.rem(f + k, n_feat), f).wait_send()

    for c in loads[:3]:
        c.wait()
    for c in loads[3:]:
        c.start()
    masked[...] = masked_rows(grad, pre)
    nodes = grad.shape[0]
    product = lax.dot_general(w_neigh[...], masked[...], NT, **HIGH)
    for owner in range(n_feat):
        neigh_send[owner] = halves_of(product, owner)
    pl.semaphore_wait(barrier, n_feat - 1 + n_edge - 1)
    start_all(neigh_copy)

    neigh[f] = neigh_send[f]
    permute[...] = permutation()
    loads[3].wait()
    loads[4].wait()
    find_chains(count_ref, col_smem, row, col, row_v, prev_v, last_v)
    places = ((row_v, row_s), (prev_v, prev_s), (last_v, last_s))
    moves = [pltpu.make_async_copy(a, b, index_sem.at[i]) for i, (a, b) in enumerate(places)]
    for c in moves:
        c.start()
    loads[5].wait()
    product = lax.dot_general(w_self[...], masked[...], NT, **HIGH)
    for owner in range(n_feat):
        back_send[owner] = halves_of(product, owner)
    loads[6].wait()
    loads[7].wait()
    for owner in range(n_feat):
        span = slice(owner * nodes, (owner + 1) * nodes)
        both = jnp.concatenate([feat[:, span].astype(F32), agg[:, span].astype(F32)], 0)
        node_send[owner] = both.astype(BF16)
    node_recv[f] = node_send[f]
    back_recv[f] = back_send[f]
    sent_all(neigh_copy)
    start_all(node_copy)
    start_all(back_copy)
    for low in range(0, n_feat, 4):
        sources = [lax.rem(f + k, n_feat) for k in range(low, low + 4)]
        for k in range(low, low + 4):
            if k > 0:
                neigh_copy(sources[k - low], sources[k - low]).wait_recv()
        build_table(sources, neigh, table, permute)
    for c in moves:
        c.wait()
    loads[8].wait()
    products(row_s, prev_s, blocks, table, sums, even, odd)

    half = packed.shape[3] // 2
    step_of = (1, -1)
    OPP, RIGHT, LEFT, OWN = range(4)
    away = {OPP: 2, RIGHT: 1, LEFT: -1, OWN: 0}

    def edge_at(dx, py):
        return lax.rem(x + dx + 4, 4) * 2 + py

    def along_x(src, dst, send_sem, recv_sem, d):
        return pltpu.make_async_remote_copy(
            src_ref=src, dst_ref=dst, send_sem=send_sem, recv_sem=recv_sem,
            device_id={"edge": edge_at(step_of[d], y)}, device_id_type=MESH,
        )

    def along_y(src, dst, send_sem, recv_sem):
        return pltpu.make_async_remote_copy(
            src_ref=src, dst_ref=dst, send_sem=send_sem, recv_sem=recv_sem,
            device_id={"edge": edge_at(0, 1 - y)}, device_id_type=MESH,
        )

    def lanes_of(h, low, high):
        return pl.ds(h * half + low, high - low)

    def sub(j):
        return pl.ds(SUBS[j][0], SUBS[j][1] - SUBS[j][0])

    def one(p, d, j):
        src = packed.at[p, OPP, :, lanes_of(d, *SUBS[j])]
        return along_x(src, one_recv.at[p, d, :, sub(j)], one_ss.at[p, d, j], one_rs.at[p, d, j], d)

    def two(p, d, j):
        src = packed.at[p, RIGHT + d, :, lanes_of(1 - d, *SUBS[j])]
        return along_x(src, two_recv.at[p, d, :, sub(j)], two_ss.at[p, d, j], two_rs.at[p, d, j], d)

    def three(p, d, j):
        return along_x(
            three_send.at[p, d, :, sub(j)], three_recv.at[p, d, :, sub(j)],
            three_ss.at[p, d, j], three_rs.at[p, d, j], d,
        )

    def y_copy(h, j):
        return along_y(y_send.at[h, :, sub(j)], y_recv.at[h, :, sub(j)], y_ss.at[h, j], y_rs.at[h, j])

    def yf_copy(i, h):
        src = packed.at[0, i, :, lanes_of(h, X_FIRST, half)]
        return along_y(src, yf_recv.at[i, h], yf_ss.at[i, h], yf_rs.at[i, h])

    def t_one_copy(d):
        return along_x(t_sum.at[OPP, d], t_one.at[d], t_one_ss.at[d], t_one_rs.at[d], d)

    def t_two_copy(d):
        return along_x(t_sum.at[RIGHT + d, 1 - d], t_two.at[d], t_two_ss.at[d], t_two_rs.at[d], d)

    def t_three_copy(d):
        return along_x(t_three_send.at[d], t_three_recv.at[d], t_three_ss.at[d], t_three_rs.at[d], d)

    both_ways = [(j, d) for j in range(2) for d in range(2)]

    def pack_to(p, i):
        pack(edge_at(away[i], 1 - y if p == 0 else y), last_s, sums, packed.at[p, i])

    pack_to(0, OPP)
    for j, d in both_ways:
        one(0, d, j).start()
    for h in range(2):
        yf_copy(OPP, h).start()
    for d in range(2):
        pack_to(0, RIGHT + d)
        for j in range(2):
            two(0, d, j).start()
        for h in range(2):
            yf_copy(RIGHT + d, h).start()
    pack_to(0, OWN)
    for h in range(2):
        yf_copy(OWN, h).start()
    pack_to(1, OPP)

    def relay(p):
        for j, d in both_ways:
            one(p, d, j).wait_recv()
            low, high = SUBS[j]
            mine = packed[p, RIGHT + d, :, d * half + low : d * half + high].astype(F32)
            three_send[p, d, :, low:high] = (mine + one_recv[p, d, :, low:high].astype(F32)).astype(BF16)
            three(p, d, j).start()

    relay(0)
    for j, d in both_ways:
        one(1, d, j).start()
    for d in range(2):
        pack_to(1, RIGHT + d)
        for j in range(2):
            two(1, d, j).start()
    pack_to(1, OWN)

    receive_all(node_copy)
    stacked = node_recv[...].reshape(n_feat * 16, nodes)
    terms[...] = jnp.dot(stacked, masked[...], **HIGH).reshape(terms.shape)
    start_all(term_copy)
    terms_recv[f] = terms[f]

    def sum_y(i):
        for h in range(2):
            yf_copy(i, h).wait_recv()
            mine = packed[1, i, :, h * half + X_FIRST : (h + 1) * half].astype(F32)
            t_sum[i, h] = (mine + yf_recv[i, h].astype(F32)).astype(BF16)

    sum_y(OPP)
    for d in range(2):
        t_one_copy(d).start()
    for d in range(2):
        sum_y(RIGHT + d)
        t_two_copy(d).start()
    sum_y(OWN)

    def arrived(p, h, low, high):
        return (
            packed[p, OWN, :, h * half + low : h * half + high].astype(F32)
            + three_recv[p, h, :, low:high].astype(F32)
            + two_recv[p, 1 - h, :, low:high].astype(F32)
        )

    for j, h in both_ways:
        two(0, 1 - h, j).wait_recv()
        three(0, h, j).wait_recv()
        y_send[h, :, SUBS[j][0] : SUBS[j][1]] = arrived(0, h, *SUBS[j]).astype(BF16)
        y_copy(h, j).start()

    relay(1)
    for d in range(2):
        t_one_copy(d).wait_recv()
        t_three_send[d] = (t_sum[RIGHT + d, d].astype(F32) + t_one[d].astype(F32)).astype(BF16)
        t_three_copy(d).start()

    receive_all(term_copy)
    total = terms_recv[0]
    for k in range(1, n_feat):
        total = total + terms_recv[k]
    term[...] = total

    def edge_term(peer, slot):
        return pltpu.make_async_remote_copy(
            src_ref=term, dst_ref=edge_recv.at[slot], send_sem=edge_ss.at[peer], recv_sem=edge_rs.at[slot],
            device_id={"edge": peer}, device_id_type=MESH,
        )

    @pl.loop(1, n_edge)
    def _(k):
        edge_term(lax.rem(e + k, n_edge), e).start()

    edge_recv[e] = term[...]
    receive_all(back_copy)

    def finish(h, low, total):
        span = nodes // 2
        for r in range(2):
            for k in range(total.shape[1] // span):
                node = r * 2 * half + h * half + low + k * span
                src, part = node // nodes, node % nodes // span
                back = back_recv[src].astype(F32)[part * 8 : part * 8 + 8]
                rows = total[r * 8 : r * 8 + 8, k * span : (k + 1) * span]
                out_ref[:, node : node + span] = (rows + back).astype(BF16)

    for j, h in both_ways:
        low, high = SUBS[j]
        two(1, 1 - h, j).wait_recv()
        three(1, h, j).wait_recv()
        y_copy(h, j).wait_recv()
        finish(h, low, arrived(1, h, low, high) + y_recv[h, :, low:high].astype(F32))
    for h in range(2):
        t_two_copy(1 - h).wait_recv()
        t_three_copy(h).wait_recv()
        finish(h, X_FIRST, t_sum[OWN, h].astype(F32) + t_three_recv[h].astype(F32) + t_two[1 - h].astype(F32))

    @pl.loop(1, n_edge)
    def _(k):
        peer = lax.rem(e + k, n_edge)
        edge_term(peer, peer).wait_recv()

    total = edge_recv[0]
    for k in range(1, n_edge):
        total = total + edge_recv[k]
    weight_ref[...] = total * factor

    for copy in (back_copy, node_copy, term_copy):
        sent_all(copy)

    @pl.loop(1, n_edge)
    def _(k):
        edge_term(lax.rem(e + k, n_edge), e).wait_send()

    for p in range(2):
        for j, d in both_ways:
            one(p, d, j).wait_send()
            two(p, d, j).wait_send()
            three(p, d, j).wait_send()
    for j, h in both_ways:
        y_copy(h, j).wait_send()
    for i in range(4):
        for h in range(2):
            yf_copy(i, h).wait_send()
    for d in range(2):
        t_one_copy(d).wait_send()
        t_two_copy(d).wait_send()
        t_three_copy(d).wait_send()


def layer(counts, row_index, col_index, w_self, w_neigh, grad_out, pre_act, feat_t, agg_t, blocks, n_feat, n_edge, factor):
    nodes, hidden = grad_out.shape
    features, slab = feat_t.shape
    slots = blocks.shape[0]
    half = slab // 4
    y_first = half - X_FIRST
    names = n_edge * slab // 64
    spots = (slots // 128, 128)
    smem = pl.BlockSpec(memory_space=pltpu.SMEM)
    vmem = pl.BlockSpec(memory_space=pltpu.VMEM)
    hbm = pl.BlockSpec(memory_space=pl.ANY)
    dma = pltpu.SemaphoreType.DMA
    ints = [spots, spots, (2, names // 128, 128)]
    small, large = (n_feat, 16, nodes // 2), (n_feat, 16, nodes)
    x_part = (2, 2, 16, X_FIRST)
    y_part = (2, 16, X_FIRST)
    return pl.pallas_call(
        functools.partial(layer_kernel, n_feat, factor),
        in_specs=[smem, smem] + [hbm] * 9,
        out_specs=[vmem] * 2,
        out_shape=[
            jax.ShapeDtypeStruct((features, slab), BF16),
            jax.ShapeDtypeStruct((2 * features, hidden), F32),
        ],
        scratch_shapes=[
            pltpu.VMEM(w_neigh.shape, BF16),
            pltpu.VMEM((nodes, hidden), BF16),
            pltpu.VMEM((nodes, hidden), BF16),
            pltpu.VMEM(spots, jnp.int32),
            pltpu.VMEM(spots, jnp.int32),
            pltpu.VMEM(w_self.shape, BF16),
            pltpu.VMEM((features, slab), BF16),
            pltpu.VMEM((features, slab), BF16),
            pltpu.VMEM(blocks.shape, BF16),
            pltpu.VMEM((nodes, hidden), BF16),
            pltpu.VMEM((128, 1024), BF16),
            pltpu.VMEM((slab // 64, 16, 256), BF16),
            pltpu.VMEM((slots // 2 + 1, 8, 128), F32),
            pltpu.VMEM((slots // 2 + 1, 8, 128), F32),
            pltpu.VMEM((256, 128), F32),
            pltpu.VMEM((256, 128), F32),
            pltpu.VMEM((2, 4, 16, 2 * half), BF16),
            *[pltpu.VMEM(i, jnp.int32) for i in ints],
            *[pltpu.SMEM(i, jnp.int32) for i in ints],
            *[pltpu.VMEM(i, BF16) for i in (small, small, small, small, large, large)],
            pltpu.VMEM((n_feat, 16, hidden), F32),
            pltpu.VMEM((n_feat, 16, hidden), F32),
            pltpu.VMEM((16, hidden), F32),
            pltpu.VMEM((n_edge, 16, hidden), F32),
            *[pltpu.VMEM(i, BF16) for i in (x_part, x_part, x_part, x_part, y_part, y_part)],
            *[pltpu.VMEM((4, 2, 16, y_first), BF16) for i in range(2)],
            *[pltpu.VMEM((2, 16, y_first), BF16) for i in range(4)],
            dma((9,)),
            dma((3,)),
            *[dma((n_feat,)) for i in range(8)],
            dma((n_edge,)),
            dma((n_edge,)),
            *[dma((2, 2, 2)) for i in range(6)],
            dma((2, 2)),
            dma((2, 2)),
            dma((4, 2)),
            dma((4, 2)),
            *[dma((2,)) for i in range(6)],
        ],
        compiler_params=pltpu.CompilerParams(collective_id=0, has_side_effects=True, vmem_limit_bytes=60 * MIB),
        name="layer",
    )(counts, col_index, row_index.reshape(spots), col_index.reshape(spots), w_self, w_neigh, grad_out, pre_act, feat_t, agg_t, blocks)


def split_kernel(out_ref, weight_ref, feat_ref, self_ref, neigh_ref):
    features = out_ref.shape[0]
    feat_ref[...] = out_ref[...]
    self_ref[...] = weight_ref[:features]
    neigh_ref[...] = weight_ref[features:]


def split(out, weights):
    features = out.shape[0]
    weight = jax.ShapeDtypeStruct((features, weights.shape[1]), F32)
    vmem = pl.BlockSpec(memory_space=pltpu.VMEM)
    return pl.pallas_call(
        split_kernel,
        in_specs=[vmem] * 2,
        out_specs=[vmem] * 3,
        out_shape=[jax.ShapeDtypeStruct(out.shape, BF16), weight, weight],
        name="split",
    )(out, weights)


def on_device(grad_out, pre_act, feat_t, agg_t, w_self, w_neigh, blocks, row_index, col_index, counts):
    n_feat = lax.axis_size("feat")
    n_edge = lax.axis_size("edge")
    slab = feat_t.shape[1]
    factor = 1.0 / math.sqrt(slab * n_edge)
    out, weights = layer(
        counts, row_index, col_index, w_self, w_neigh, grad_out, pre_act, feat_t, agg_t, blocks, n_feat, n_edge, factor
    )
    return tuple(split(out, weights))


def solution(mesh):
    in_specs = (
        P(("edge", "feat"), None),
        P(("edge", "feat"), None),
        P("feat", "edge"),
        P("feat", "edge"),
        P(),
        P(),
        P("edge", None),
        P("edge"),
        P("edge"),
        P("edge"),
    )
    out_specs = (P("feat", "edge"), P("feat", None), P("feat", None))
    return jax.shard_map(
        on_device, mesh=mesh, in_specs=in_specs, out_specs=out_specs, check_vma=False
    )
```

```python
import functools
import math

import jax
import jax.numpy as jnp
from jax import lax
from jax.experimental import pallas as pl
from jax.experimental.pallas import tpu as pltpu
from jax.sharding import PartitionSpec as P

MESH = pl.DeviceIdType.MESH
MIB = 2**20
F32 = jnp.float32
BF16 = jnp.bfloat16
HIGH = dict(preferred_element_type=F32)
NT = (((1,), (1,)), ((), ()))


def masked_rows(grad_ref, pre_ref):
    return jnp.where(pre_ref[...] > 0, grad_ref[...], jnp.zeros_like(grad_ref))


def halves_of(product, owner):
    nodes = product.shape[1]
    rows = product[owner * 8 : owner * 8 + 8]
    both = jnp.concatenate([rows[:, : nodes // 2], rows[:, nodes // 2 :]], 0)
    return both.astype(BF16)


def find_chains(count_ref, col_smem, row_ref, col_ref, row_out, prev_out, last_out):
    slots = row_ref.shape[0] * 128
    count = count_ref[0]

    def count_up(shape):
        return lax.broadcasted_iota(jnp.int32, shape, 0) * 128 + lax.broadcasted_iota(jnp.int32, shape, 1)

    spot = count_up(row_ref.shape)
    alive = spot < count
    row_out[...] = jnp.where(alive, row_ref[...], 0)
    cols = [jnp.where(alive & (spot % 2 == k), col_ref[...], -2) for k in range(2)]
    names = count_up(last_out.shape[1:])

    def body(i, carry):
        prev, last = carry[0], list(carry[1:])
        for u in range(32):
            s = i * 32 + u
            place = i * 16 + u // 2
            c = jnp.where(s < count, col_smem[s], -1)
            prev = jnp.where((cols[u % 2] == c) & (spot > s), place, prev)
            last[u % 2] = jnp.where(names == c, place, last[u % 2])
        return prev, *last

    none = [jnp.full(n, slots // 2, jnp.int32) for n in (row_ref.shape, names.shape, names.shape)]
    prev, *last = lax.fori_loop(0, slots // 32, body, tuple(none))
    prev_out[...] = prev
    for k in range(2):
        last_out[k] = last[k]


def build_table(sources, neigh, table, permute_ref):
    tiles = neigh.shape[2] // 128
    x = jnp.concatenate([neigh[i, :, t * 128 : (t + 1) * 128] for i in sources for t in range(tiles)], 0)
    for b in range(2):
        y = jnp.dot(x, permute_ref[:, b * 512 : (b + 1) * 512], **HIGH)
        for n, i in enumerate(sources):
            for t in range(tiles):
                for h in range(2):
                    at = (n * tiles + t) * 16 + h * 8
                    both = jnp.concatenate([y[at : at + 8, :256], y[at : at + 8, 256:]], 0)
                    table[i * (4 * tiles) + h * 2 * tiles + 2 * t + b] = both.astype(BF16)


def permutation():
    place = lax.broadcasted_iota(jnp.int32, (128, 1024), 1)
    source = place // 512 * 64 + (place % 256) // 8 * 2 + place // 256 % 2
    node = lax.broadcasted_iota(jnp.int32, (128, 1024), 0)
    return jnp.where(source == node, 1.0, 0.0).astype(BF16)


def products(row_smem, prev_smem, blocks, table, sums, even, odd):
    slots = blocks.shape[0]
    steps = slots // 128
    lane = lax.broadcasted_iota(jnp.int32, (8, 128), 1)
    own = lax.broadcasted_iota(jnp.int32, (16, 256), 1) % 8
    for k in range(2):
        sums[k][slots // 2] = jnp.zeros((8, 128), F32)

    def product(step, g, dst):
        rows = pl.ds(pl.multiple_of(step * 128 + g * 16, 16), 16)
        tiles = [blocks[rows, t * 128 : (t + 1) * 128].astype(F32) for t in range(32)]
        for h in range(2):
            left = []
            for q in range(8):
                mine = table[row_smem[step, g * 16 + h * 8 + q]]
                left.append(jnp.where(own == q, mine, jnp.zeros((16, 256), BF16)))
            right = jnp.concatenate([t[h * 8 : h * 8 + 8] for t in tiles], 0).astype(BF16)
            dst[h * 128 : h * 128 + 128] = jnp.dot(jnp.concatenate(left, 0), right, **HIGH)

    def collect(step, g, src):
        for q in range(16):
            before = sums[q % 2][prev_smem[step, g * 16 + q]]
            v = jnp.where(lane < 64, src[q * 16 : q * 16 + 8], src[q * 16 + 8 : q * 16 + 16])
            sums[q % 2][step * 64 + g * 8 + q // 2] = v + before

    kept = (even, odd)
    product(0, 0, even)

    @pl.loop(0, steps)
    def _(step):
        for g in range(8):
            if g < 7:
                product(step, g + 1, kept[(g + 1) % 2])
            else:
                product(jnp.minimum(step + 1, steps - 1), 0, even)
            collect(step, g, kept[g % 2])


def pack(e, last_smem, sums, out_ref):
    rows = out_ref.shape[1] // 64 // 128
    lane = lax.broadcasted_iota(jnp.int32, (8, 128), 1)
    for k in range(rows):
        for u in range(64):
            two = []
            for h in range(2):
                r = (e * 2 + h) * rows + k
                a, b = [sums[0][last_smem[0, r, c]] + sums[1][last_smem[1, r, c]] for c in (2 * u, 2 * u + 1)]
                two.append(jnp.where(lane < 64, a, b) + pltpu.roll(jnp.where(lane < 64, b, a), 64, 1))
            low = (k * 64 + u) * 128
            out_ref[:, low : low + 128] = jnp.concatenate(two, 0).astype(BF16)


X_FIRST = 5120
SUBS = ((0, 2048), (2048, 5120))


def layer_kernel(
    n_feat, factor, count_ref, col_smem, row_hbm, col_hbm, w_self_hbm, w_neigh_hbm, grad_hbm, pre_hbm, feat_hbm, agg_hbm,
    blocks_hbm, out_ref, weight_ref,
    w_neigh, grad, pre, row, col, w_self, feat, agg, blocks, masked, permute, table, sums_even, sums_odd, even, odd, packed,
    row_v, prev_v, last_v, row_s, prev_s, last_s,
    neigh_send, neigh, back_send, back_recv, node_send, node_recv, terms, terms_recv, term, edge_recv,
    one_recv, two_recv, three_send, three_recv, y_send, y_recv,
    yf_recv, t_sum, t_one, t_two, t_three_send, t_three_recv,
    load_sem, index_sem, neigh_ss, neigh_rs, back_ss, back_rs, node_ss, node_rs, term_ss, term_rs, edge_ss, edge_rs,
    one_ss, one_rs, two_ss, two_rs, three_ss, three_rs, y_ss, y_rs,
    yf_ss, yf_rs, t_one_ss, t_one_rs, t_two_ss, t_two_rs, t_three_ss, t_three_rs,
):
    f = lax.axis_index("feat")
    e = lax.axis_index("edge")
    x, y = e // 2, e % 2
    n_edge = 8
    sums = (sums_even, sums_odd)
    barrier = pltpu.get_barrier_semaphore()

    @pl.loop(1, n_feat)
    def _(k):
        peer = {"feat": lax.rem(f + k, n_feat)}
        pl.semaphore_signal(barrier, inc=1, device_id=peer, device_id_type=MESH)

    @pl.loop(1, n_edge)
    def _(k):
        peer = {"edge": lax.rem(e + k, n_edge)}
        pl.semaphore_signal(barrier, inc=1, device_id=peer, device_id_type=MESH)

    pairs = (
        (w_neigh_hbm, w_neigh), (grad_hbm, grad), (pre_hbm, pre), (row_hbm, row), (col_hbm, col),
        (w_self_hbm, w_self), (feat_hbm, feat), (agg_hbm, agg), (blocks_hbm, blocks),
    )
    loads = [pltpu.make_async_copy(a, b, load_sem.at[i]) for i, (a, b) in enumerate(pairs)]
    for c in loads[:3]:
        c.start()

    def all_of(ref, sem):
        return pltpu.make_async_copy(ref, ref, sem)

    def start_all(src, dst, send_sem, recv_sem):
        @pl.loop(1, n_feat)
        def _(k):
            peer = lax.rem(f + k, n_feat)
            pltpu.make_async_remote_copy(
                src_ref=src.at[peer], dst_ref=dst.at[f], send_sem=send_sem, recv_sem=recv_sem,
                device_id={"feat": peer}, device_id_type=MESH,
            ).start()

    def await_all(ref, sem):
        all_of(ref.at[pl.ds(0, n_feat - 1)], sem).wait()

    for c in loads[:3]:
        c.wait()
    for c in loads[3:]:
        c.start()
    masked[...] = masked_rows(grad, pre)
    nodes = grad.shape[0]
    product = lax.dot_general(w_neigh[...], masked[...], NT, **HIGH)
    for owner in range(n_feat):
        neigh_send[owner] = halves_of(product, owner)
    pl.semaphore_wait(barrier, n_feat - 1 + n_edge - 1)
    start_all(neigh_send, neigh, neigh_ss, neigh_rs)

    neigh[f] = neigh_send[f]
    permute[...] = permutation()
    loads[3].wait()
    loads[4].wait()
    find_chains(count_ref, col_smem, row, col, row_v, prev_v, last_v)
    places = ((row_v, row_s), (prev_v, prev_s), (last_v, last_s))
    moves = [pltpu.make_async_copy(a, b, index_sem.at[i]) for i, (a, b) in enumerate(places)]
    for c in moves:
        c.start()
    loads[5].wait()
    product = lax.dot_general(w_self[...], masked[...], NT, **HIGH)
    for owner in range(n_feat):
        back_send[owner] = halves_of(product, owner)
    loads[6].wait()
    loads[7].wait()
    for owner in range(n_feat):
        span = slice(owner * nodes, (owner + 1) * nodes)
        both = jnp.concatenate([feat[:, span].astype(F32), agg[:, span].astype(F32)], 0)
        node_send[owner] = both.astype(BF16)
    node_recv[f] = node_send[f]
    back_recv[f] = back_send[f]
    await_all(neigh_send, neigh_ss)
    start_all(node_send, node_recv, node_ss, node_rs)
    start_all(back_send, back_recv, back_ss, back_rs)
    await_all(neigh, neigh_rs)
    for low in range(0, n_feat, 4):
        sources = [lax.rem(f + k, n_feat) for k in range(low, low + 4)]
        build_table(sources, neigh, table, permute)
    for c in moves:
        c.wait()
    loads[8].wait()
    products(row_s, prev_s, blocks, table, sums, even, odd)

    half = packed.shape[3] // 2
    step_of = (1, -1)
    OPP, RIGHT, LEFT, OWN = range(4)

    def edge_at(dx, py):
        return lax.rem(x + dx + 4, 4) * 2 + py

    def along_x(src, dst, send_sem, recv_sem, d):
        return pltpu.make_async_remote_copy(
            src_ref=src, dst_ref=dst, send_sem=send_sem, recv_sem=recv_sem,
            device_id={"edge": edge_at(step_of[d], y)}, device_id_type=MESH,
        )

    def along_y(src, dst, send_sem, recv_sem):
        return pltpu.make_async_remote_copy(
            src_ref=src, dst_ref=dst, send_sem=send_sem, recv_sem=recv_sem,
            device_id={"edge": edge_at(0, 1 - y)}, device_id_type=MESH,
        )

    def lanes_of(h, low, high):
        return pl.ds(h * half + low, high - low)

    def sub(j):
        return pl.ds(SUBS[j][0], SUBS[j][1] - SUBS[j][0])

    def one(p, d, j):
        src = packed.at[p, OPP, :, lanes_of(d, *SUBS[j])]
        return along_x(src, one_recv.at[p, d, :, sub(j)], one_ss, one_rs.at[p, d, j], d)

    def two(p, d, j):
        src = packed.at[p, RIGHT + d, :, lanes_of(1 - d, *SUBS[j])]
        return along_x(src, two_recv.at[p, d, :, sub(j)], two_ss, two_rs.at[p, d, j], d)

    def three(p, d, j):
        return along_x(
            three_send.at[p, d, :, sub(j)], three_recv.at[p, d, :, sub(j)],
            three_ss, three_rs.at[p, d, j], d,
        )

    def y_copy(h, j):
        return along_y(y_send.at[h, :, sub(j)], y_recv.at[h, :, sub(j)], y_ss, y_rs.at[h, j])

    def yf_copy(i, h):
        src = packed.at[0, i, :, lanes_of(h, X_FIRST, half)]
        return along_y(src, yf_recv.at[i, h], yf_ss, yf_rs.at[i])

    def t_one_copy(d):
        return along_x(t_sum.at[OPP, d], t_one.at[d], t_one_ss, t_one_rs.at[d], d)

    def t_two_copy(d):
        return along_x(t_sum.at[RIGHT + d, 1 - d], t_two.at[d], t_two_ss, t_two_rs.at[d], d)

    def t_three_copy(d):
        return along_x(t_three_send.at[d], t_three_recv.at[d], t_three_ss, t_three_rs.at[d], d)

    both_ways = [(j, d) for j in range(2) for d in range(2)]

    def pack_to(t):
        p, i = t // 4, t % 4
        dx = lax.rem(2 + 3 * i + (i // 2) * (3 + 2 * (i % 2)), 4)
        py = (1 - p) * (1 - y) + p * y
        pack(lax.rem(x + dx, 4) * 2 + py, last_s, sums, packed.at[p, i])

    @pl.loop(0, 5)
    def _(t):
        pack_to(t)

        @pl.when(t == OPP)
        def _():
            for j, d in both_ways:
                one(0, d, j).start()

        for d in range(2):

            @pl.when(t == RIGHT + d)
            def _():
                for j in range(2):
                    two(0, d, j).start()

        @pl.when(t < 4)
        def _():
            for h in range(2):
                yf_copy(t, h).start()

    def relay(p):
        for j, d in both_ways:
            one(p, d, j).wait_recv()
            low, high = SUBS[j]
            mine = packed[p, RIGHT + d, :, d * half + low : d * half + high].astype(F32)
            three_send[p, d, :, low:high] = (mine + one_recv[p, d, :, low:high].astype(F32)).astype(BF16)
            three(p, d, j).start()

    relay(0)
    for j, d in both_ways:
        one(1, d, j).start()

    @pl.loop(5, 8)
    def _(t):
        pack_to(t)
        for d in range(2):

            @pl.when(t == 4 + RIGHT + d)
            def _():
                for j in range(2):
                    two(1, d, j).start()


    await_all(node_recv, node_rs)
    stacked = node_recv[...].reshape(n_feat * 16, nodes)
    terms[...] = jnp.dot(stacked, masked[...], **HIGH).reshape(terms.shape)
    start_all(terms, terms_recv, term_ss, term_rs)
    terms_recv[f] = terms[f]

    def sum_y(i):
        all_of(yf_recv.at[i], yf_rs.at[i]).wait()
        for h in range(2):
            mine = packed[1, i, :, h * half + X_FIRST : (h + 1) * half].astype(F32)
            t_sum[i, h] = (mine + yf_recv[i, h].astype(F32)).astype(BF16)

    sum_y(OPP)
    for d in range(2):
        t_one_copy(d).start()
    for d in range(2):
        sum_y(RIGHT + d)
        t_two_copy(d).start()
    sum_y(OWN)

    def arrived(p, h, low, high):
        return (
            packed[p, OWN, :, h * half + low : h * half + high].astype(F32)
            + three_recv[p, h, :, low:high].astype(F32)
            + two_recv[p, 1 - h, :, low:high].astype(F32)
        )

    for j, h in both_ways:
        two(0, 1 - h, j).wait_recv()
        three(0, h, j).wait_recv()
        y_send[h, :, SUBS[j][0] : SUBS[j][1]] = arrived(0, h, *SUBS[j]).astype(BF16)
        y_copy(h, j).start()

    relay(1)
    for d in range(2):
        t_one_copy(d).wait_recv()
        t_three_send[d] = (t_sum[RIGHT + d, d].astype(F32) + t_one[d].astype(F32)).astype(BF16)
        t_three_copy(d).start()

    await_all(terms_recv, term_rs)
    total = terms_recv[0]
    for k in range(1, n_feat):
        total = total + terms_recv[k]
    term[...] = total

    @pl.loop(1, n_edge)
    def _(k):
        peer = lax.rem(e + k, n_edge)
        pltpu.make_async_remote_copy(
            src_ref=term, dst_ref=edge_recv.at[e], send_sem=edge_ss, recv_sem=edge_rs,
            device_id={"edge": peer}, device_id_type=MESH,
        ).start()

    edge_recv[e] = term[...]
    await_all(back_recv, back_rs)

    def finish(h, low, total):
        span = nodes // 2
        for r in range(2):
            for k in range(total.shape[1] // span):
                node = r * 2 * half + h * half + low + k * span
                src, part = node // nodes, node % nodes // span
                back = back_recv[src].astype(F32)[part * 8 : part * 8 + 8]
                rows = total[r * 8 : r * 8 + 8, k * span : (k + 1) * span]
                out_ref[:, node : node + span] = (rows + back).astype(BF16)

    for j, h in both_ways:
        low, high = SUBS[j]
        two(1, 1 - h, j).wait_recv()
        three(1, h, j).wait_recv()
        y_copy(h, j).wait_recv()
        finish(h, low, arrived(1, h, low, high) + y_recv[h, :, low:high].astype(F32))
    for h in range(2):
        t_two_copy(1 - h).wait_recv()
        t_three_copy(h).wait_recv()
        finish(h, X_FIRST, t_sum[OWN, h].astype(F32) + t_three_recv[h].astype(F32) + t_two[1 - h].astype(F32))

    edge_bytes = edge_recv.at[pl.ds(0, n_edge - 1)]
    all_of(edge_bytes, edge_rs).wait()
    total = edge_recv[0]
    for k in range(1, n_edge):
        total = total + edge_recv[k]
    weight_ref[...] = total * factor

    await_all(back_send, back_ss)
    await_all(node_send, node_ss)
    await_all(terms, term_ss)

    sent = (
        (edge_bytes, edge_ss), (one_recv, one_ss), (two_recv, two_ss), (three_send, three_ss), (y_send, y_ss),
        (yf_recv, yf_ss), (t_one, t_one_ss), (t_two, t_two_ss), (t_three_send, t_three_ss),
    )
    for ref, sem in sent:
        all_of(ref, sem).wait()


def layer(counts, row_index, col_index, w_self, w_neigh, grad_out, pre_act, feat_t, agg_t, blocks, n_feat, n_edge, factor):
    nodes, hidden = grad_out.shape
    features, slab = feat_t.shape
    slots = blocks.shape[0]
    half = slab // 4
    y_first = half - X_FIRST
    names = n_edge * slab // 64
    spots = (slots // 128, 128)
    smem = pl.BlockSpec(memory_space=pltpu.SMEM)
    vmem = pl.BlockSpec(memory_space=pltpu.VMEM)
    hbm = pl.BlockSpec(memory_space=pl.ANY)
    dma = pltpu.SemaphoreType.DMA
    ints = [spots, spots, (2, names // 128, 128)]
    small, large = (n_feat, 16, nodes // 2), (n_feat, 16, nodes)
    x_part = (2, 2, 16, X_FIRST)
    y_part = (2, 16, X_FIRST)
    return pl.pallas_call(
        functools.partial(layer_kernel, n_feat, factor),
        in_specs=[smem, smem] + [hbm] * 9,
        out_specs=[vmem] * 2,
        out_shape=[
            jax.ShapeDtypeStruct((features, slab), BF16),
            jax.ShapeDtypeStruct((2 * features, hidden), F32),
        ],
        scratch_shapes=[
            pltpu.VMEM(w_neigh.shape, BF16),
            pltpu.VMEM((nodes, hidden), BF16),
            pltpu.VMEM((nodes, hidden), BF16),
            pltpu.VMEM(spots, jnp.int32),
            pltpu.VMEM(spots, jnp.int32),
            pltpu.VMEM(w_self.shape, BF16),
            pltpu.VMEM((features, slab), BF16),
            pltpu.VMEM((features, slab), BF16),
            pltpu.VMEM(blocks.shape, BF16),
            pltpu.VMEM((nodes, hidden), BF16),
            pltpu.VMEM((128, 1024), BF16),
            pltpu.VMEM((slab // 64, 16, 256), BF16),
            pltpu.VMEM((slots // 2 + 1, 8, 128), F32),
            pltpu.VMEM((slots // 2 + 1, 8, 128), F32),
            pltpu.VMEM((256, 128), F32),
            pltpu.VMEM((256, 128), F32),
            pltpu.VMEM((2, 4, 16, 2 * half), BF16),
            *[pltpu.VMEM(i, jnp.int32) for i in ints],
            *[pltpu.SMEM(i, jnp.int32) for i in ints],
            *[pltpu.VMEM(i, BF16) for i in (small, small, small, small, large, large)],
            pltpu.VMEM((n_feat, 16, hidden), F32),
            pltpu.VMEM((n_feat, 16, hidden), F32),
            pltpu.VMEM((16, hidden), F32),
            pltpu.VMEM((n_edge, 16, hidden), F32),
            *[pltpu.VMEM(i, BF16) for i in (x_part, x_part, x_part, x_part, y_part, y_part)],
            *[pltpu.VMEM((4, 2, 16, y_first), BF16) for i in range(2)],
            *[pltpu.VMEM((2, 16, y_first), BF16) for i in range(4)],
            dma((9,)),
            dma((3,)),
            *[dma] * 10,
            *[dma, dma((2, 2, 2))] * 3,
            *[dma, dma((2, 2))],
            *[dma, dma((4,))],
            *[dma, dma((2,))] * 3,
        ],
        compiler_params=pltpu.CompilerParams(collective_id=0, has_side_effects=True, vmem_limit_bytes=60 * MIB),
        name="layer",
    )(counts, col_index, row_index.reshape(spots), col_index.reshape(spots), w_self, w_neigh, grad_out, pre_act, feat_t, agg_t, blocks)


def split_kernel(out_ref, weight_ref, feat_ref, self_ref, neigh_ref):
    features = out_ref.shape[0]
    feat_ref[...] = out_ref[...]
    self_ref[...] = weight_ref[:features]
    neigh_ref[...] = weight_ref[features:]


def split(out, weights):
    features = out.shape[0]
    weight = jax.ShapeDtypeStruct((features, weights.shape[1]), F32)
    vmem = pl.BlockSpec(memory_space=pltpu.VMEM)
    return pl.pallas_call(
        split_kernel,
        in_specs=[vmem] * 2,
        out_specs=[vmem] * 3,
        out_shape=[jax.ShapeDtypeStruct(out.shape, BF16), weight, weight],
        name="split",
    )(out, weights)


def on_device(grad_out, pre_act, feat_t, agg_t, w_self, w_neigh, blocks, row_index, col_index, counts):
    n_feat = lax.axis_size("feat")
    n_edge = lax.axis_size("edge")
    slab = feat_t.shape[1]
    factor = 1.0 / math.sqrt(slab * n_edge)
    out, weights = layer(
        counts, row_index, col_index, w_self, w_neigh, grad_out, pre_act, feat_t, agg_t, blocks, n_feat, n_edge, factor
    )
    return tuple(split(out, weights))


def solution(mesh):
    in_specs = (
        P(("edge", "feat"), None),
        P(("edge", "feat"), None),
        P("feat", "edge"),
        P("feat", "edge"),
        P(),
        P(),
        P("edge", None),
        P("edge"),
        P("edge"),
        P("edge"),
    )
    out_specs = (P("feat", "edge"), P("feat", None), P("feat", None))
    return jax.shard_map(
        on_device, mesh=mesh, in_specs=in_specs, out_specs=out_specs, check_vma=False
    )
```

```python
import functools
import math

import jax
import jax.numpy as jnp
from jax import lax
from jax.experimental import pallas as pl
from jax.experimental.pallas import tpu as pltpu
from jax.sharding import PartitionSpec as P

MESH = pl.DeviceIdType.MESH
MIB = 2**20
F32 = jnp.float32
BF16 = jnp.bfloat16
HIGH = dict(preferred_element_type=F32)
NT = (((1,), (1,)), ((), ()))


def masked_rows(grad_ref, pre_ref):
    return jnp.where(pre_ref[...] > 0, grad_ref[...], jnp.zeros_like(grad_ref))


def halves_of(product, owner):
    nodes = product.shape[1]
    rows = product[owner * 8 : owner * 8 + 8]
    both = jnp.concatenate([rows[:, : nodes // 2], rows[:, nodes // 2 :]], 0)
    return both.astype(BF16)


def find_chains(count_ref, col_smem, row_ref, col_ref, row_out, prev_out, last_out):
    slots = row_ref.shape[0] * 128
    count = count_ref[0]

    def count_up(shape):
        return lax.broadcasted_iota(jnp.int32, shape, 0) * 128 + lax.broadcasted_iota(jnp.int32, shape, 1)

    spot = count_up(row_ref.shape)
    alive = spot < count
    row_out[...] = jnp.where(alive, row_ref[...], 0)
    cols = [jnp.where(alive & (spot % 2 == k), col_ref[...], -2) for k in range(2)]
    names = count_up(last_out.shape[1:])

    def body(i, carry):
        prev, last = carry[0], list(carry[1:])
        for u in range(32):
            s = i * 32 + u
            place = i * 16 + u // 2
            c = jnp.where(s < count, col_smem[s], -1)
            prev = jnp.where((cols[u % 2] == c) & (spot > s), place, prev)
            last[u % 2] = jnp.where(names == c, place, last[u % 2])
        return prev, *last

    none = [jnp.full(n, slots // 2, jnp.int32) for n in (row_ref.shape, names.shape, names.shape)]
    prev, *last = lax.fori_loop(0, slots // 32, body, tuple(none))
    prev_out[...] = prev
    for k in range(2):
        last_out[k] = last[k]


def build_table(sources, neigh, table, permute_ref):
    tiles = neigh.shape[2] // 128
    x = jnp.concatenate([neigh[i, :, t * 128 : (t + 1) * 128] for i in sources for t in range(tiles)], 0)
    for b in range(2):
        y = jnp.dot(x, permute_ref[:, b * 512 : (b + 1) * 512], **HIGH)
        for n, i in enumerate(sources):
            for t in range(tiles):
                for h in range(2):
                    at = (n * tiles + t) * 16 + h * 8
                    both = jnp.concatenate([y[at : at + 8, :256], y[at : at + 8, 256:]], 0)
                    table[i * (4 * tiles) + h * 2 * tiles + 2 * t + b] = both.astype(BF16)


def permutation():
    place = lax.broadcasted_iota(jnp.int32, (128, 1024), 1)
    source = place // 512 * 64 + (place % 256) // 8 * 2 + place // 256 % 2
    node = lax.broadcasted_iota(jnp.int32, (128, 1024), 0)
    return jnp.where(source == node, 1.0, 0.0).astype(BF16)


def products(row_smem, prev_smem, blocks, table, sums, even, odd):
    slots = blocks.shape[0]
    steps = slots // 128
    lane = lax.broadcasted_iota(jnp.int32, (8, 128), 1)
    own = lax.broadcasted_iota(jnp.int32, (16, 256), 1) % 8
    for k in range(2):
        sums[k][slots // 2] = jnp.zeros((8, 128), F32)

    def product(step, g, dst):
        rows = pl.ds(pl.multiple_of(step * 128 + g * 16, 16), 16)
        tiles = [blocks[rows, t * 128 : (t + 1) * 128].astype(F32) for t in range(32)]
        for h in range(2):
            left = []
            for q in range(8):
                mine = table[row_smem[step, g * 16 + h * 8 + q]]
                left.append(jnp.where(own == q, mine, jnp.zeros((16, 256), BF16)))
            right = jnp.concatenate([t[h * 8 : h * 8 + 8] for t in tiles], 0).astype(BF16)
            dst[h * 128 : h * 128 + 128] = jnp.dot(jnp.concatenate(left, 0), right, **HIGH)

    def collect(step, g, src):
        for q in range(16):
            before = sums[q % 2][prev_smem[step, g * 16 + q]]
            v = jnp.where(lane < 64, src[q * 16 : q * 16 + 8], src[q * 16 + 8 : q * 16 + 16])
            sums[q % 2][step * 64 + g * 8 + q // 2] = v + before

    kept = (even, odd)
    product(0, 0, even)

    @pl.loop(0, steps)
    def _(step):
        for g in range(8):
            if g < 7:
                product(step, g + 1, kept[(g + 1) % 2])
            else:
                product(jnp.minimum(step + 1, steps - 1), 0, even)
            collect(step, g, kept[g % 2])


def pack(e, last_smem, sums, out_ref):
    rows = out_ref.shape[1] // 64 // 128
    lane = lax.broadcasted_iota(jnp.int32, (8, 128), 1)
    for k in range(rows):
        for u in range(64):
            two = []
            for h in range(2):
                r = (e * 2 + h) * rows + k
                a, b = [sums[0][last_smem[0, r, c]] + sums[1][last_smem[1, r, c]] for c in (2 * u, 2 * u + 1)]
                two.append(jnp.where(lane < 64, a, b) + pltpu.roll(jnp.where(lane < 64, b, a), 64, 1))
            low = (k * 64 + u) * 128
            out_ref[:, low : low + 128] = jnp.concatenate(two, 0).astype(BF16)


X_FIRST = 5632
SUBS = ((0, 2560), (2560, 5632))


def layer_kernel(
    n_feat, factor, count_ref, col_smem, row_hbm, col_hbm, w_self_hbm, w_neigh_hbm, grad_hbm, pre_hbm, feat_hbm, agg_hbm,
    blocks_hbm, out_ref, weight_ref,
    w_neigh, grad, pre, row, col, w_self, feat, agg, blocks, masked, permute, table, sums_even, sums_odd, even, odd, packed,
    row_v, prev_v, last_v, row_s, prev_s, last_s,
    neigh_send, neigh, back_send, back_recv, node_send, node_recv, terms, terms_recv, term, edge_recv,
    one_recv, two_recv, three_send, three_recv, y_send, y_recv,
    yf_recv, t_sum, t_one, t_two, t_three_send, t_three_recv,
    load_sem, index_sem, neigh_ss, neigh_rs, back_ss, back_rs, node_ss, node_rs, term_ss, term_rs, edge_ss, edge_rs,
    one_ss, one_rs, two_ss, two_rs, three_ss, three_rs, y_ss, y_rs,
    yf_ss, yf_rs, t_one_ss, t_one_rs, t_two_ss, t_two_rs, t_three_ss, t_three_rs,
):
    f = lax.axis_index("feat")
    e = lax.axis_index("edge")
    x, y = e // 2, e % 2
    n_edge = 8
    sums = (sums_even, sums_odd)
    barrier = pltpu.get_barrier_semaphore()

    @pl.loop(1, n_feat)
    def _(k):
        peer = {"feat": lax.rem(f + k, n_feat)}
        pl.semaphore_signal(barrier, inc=1, device_id=peer, device_id_type=MESH)

    @pl.loop(1, n_edge)
    def _(k):
        peer = {"edge": lax.rem(e + k, n_edge)}
        pl.semaphore_signal(barrier, inc=1, device_id=peer, device_id_type=MESH)

    pairs = (
        (w_neigh_hbm, w_neigh), (grad_hbm, grad), (pre_hbm, pre), (row_hbm, row), (col_hbm, col),
        (w_self_hbm, w_self), (feat_hbm, feat), (agg_hbm, agg), (blocks_hbm, blocks),
    )
    loads = [pltpu.make_async_copy(a, b, load_sem.at[i]) for i, (a, b) in enumerate(pairs)]
    for c in loads[:3]:
        c.start()

    def all_of(ref, sem):
        return pltpu.make_async_copy(ref, ref, sem)

    def start_all(src, dst, send_sem, recv_sem):
        @pl.loop(1, n_feat)
        def _(k):
            peer = lax.rem(f + k, n_feat)
            pltpu.make_async_remote_copy(
                src_ref=src.at[peer], dst_ref=dst.at[f], send_sem=send_sem, recv_sem=recv_sem,
                device_id={"feat": peer}, device_id_type=MESH,
            ).start()

    def await_all(ref, sem):
        all_of(ref.at[pl.ds(0, n_feat - 1)], sem).wait()

    for c in loads[:3]:
        c.wait()
    for c in loads[3:]:
        c.start()
    masked[...] = masked_rows(grad, pre)
    nodes = grad.shape[0]
    product = lax.dot_general(w_neigh[...], masked[...], NT, **HIGH)
    for owner in range(n_feat):
        neigh_send[owner] = halves_of(product, owner)
    pl.semaphore_wait(barrier, n_feat - 1 + n_edge - 1)
    start_all(neigh_send, neigh, neigh_ss, neigh_rs)

    neigh[f] = neigh_send[f]
    permute[...] = permutation()
    loads[3].wait()
    loads[4].wait()
    find_chains(count_ref, col_smem, row, col, row_v, prev_v, last_v)
    places = ((row_v, row_s), (prev_v, prev_s), (last_v, last_s))
    moves = [pltpu.make_async_copy(a, b, index_sem.at[i]) for i, (a, b) in enumerate(places)]
    for c in moves:
        c.start()
    loads[5].wait()
    product = lax.dot_general(w_self[...], masked[...], NT, **HIGH)
    for owner in range(n_feat):
        back_send[owner] = halves_of(product, owner)
    loads[6].wait()
    loads[7].wait()
    for owner in range(n_feat):
        span = slice(owner * nodes, (owner + 1) * nodes)
        both = jnp.concatenate([feat[:, span].astype(F32), agg[:, span].astype(F32)], 0)
        node_send[owner] = both.astype(BF16)
    node_recv[f] = node_send[f]
    back_recv[f] = back_send[f]
    await_all(neigh_send, neigh_ss)
    start_all(node_send, node_recv, node_ss, node_rs)
    start_all(back_send, back_recv, back_ss, back_rs)
    await_all(neigh, neigh_rs)
    for low in range(0, n_feat, 4):
        sources = [lax.rem(f + k, n_feat) for k in range(low, low + 4)]
        build_table(sources, neigh, table, permute)
    for c in moves:
        c.wait()
    loads[8].wait()
    products(row_s, prev_s, blocks, table, sums, even, odd)

    half = packed.shape[3] // 2
    step_of = (1, -1)
    OPP, RIGHT, LEFT, OWN = range(4)

    def edge_at(dx, py):
        return lax.rem(x + dx + 4, 4) * 2 + py

    def along_x(src, dst, send_sem, recv_sem, d):
        return pltpu.make_async_remote_copy(
            src_ref=src, dst_ref=dst, send_sem=send_sem, recv_sem=recv_sem,
            device_id={"edge": edge_at(step_of[d], y)}, device_id_type=MESH,
        )

    def along_y(src, dst, send_sem, recv_sem):
        return pltpu.make_async_remote_copy(
            src_ref=src, dst_ref=dst, send_sem=send_sem, recv_sem=recv_sem,
            device_id={"edge": edge_at(0, 1 - y)}, device_id_type=MESH,
        )

    def lanes_of(h, low, high):
        return pl.ds(h * half + low, high - low)

    def sub(j):
        return pl.ds(SUBS[j][0], SUBS[j][1] - SUBS[j][0])

    def one(p, d, j):
        src = packed.at[p, OPP, :, lanes_of(d, *SUBS[j])]
        return along_x(src, one_recv.at[p, d, :, sub(j)], one_ss, one_rs.at[p, d, j], d)

    def two(p, d, j):
        src = packed.at[p, RIGHT + d, :, lanes_of(1 - d, *SUBS[j])]
        return along_x(src, two_recv.at[p, d, :, sub(j)], two_ss, two_rs.at[p, d, j], d)

    def three(p, d, j):
        return along_x(
            three_send.at[p, d, :, sub(j)], three_recv.at[p, d, :, sub(j)],
            three_ss, three_rs.at[p, d, j], d,
        )

    def y_copy(h, j):
        return along_y(y_send.at[h, :, sub(j)], y_recv.at[h, :, sub(j)], y_ss, y_rs.at[h, j])

    def yf_copy(i, h):
        src = packed.at[0, i, :, lanes_of(h, X_FIRST, half)]
        return along_y(src, yf_recv.at[i, h], yf_ss, yf_rs.at[i])

    def t_one_copy(d):
        return along_x(t_sum.at[OPP, d], t_one.at[d], t_one_ss, t_one_rs.at[d], d)

    def t_two_copy(d):
        return along_x(t_sum.at[RIGHT + d, 1 - d], t_two.at[d], t_two_ss, t_two_rs.at[d], d)

    def t_three_copy(d):
        return along_x(t_three_send.at[d], t_three_recv.at[d], t_three_ss, t_three_rs.at[d], d)

    both_ways = [(j, d) for j in range(2) for d in range(2)]

    def pack_to(t):
        p, i = t // 4, t % 4
        dx = lax.rem(2 + 3 * i + (i // 2) * (3 + 2 * (i % 2)), 4)
        py = (1 - p) * (1 - y) + p * y
        pack(lax.rem(x + dx, 4) * 2 + py, last_s, sums, packed.at[p, i])

    @pl.loop(0, 5)
    def _(t):
        pack_to(t)

        @pl.when(t == OPP)
        def _():
            for j, d in both_ways:
                one(0, d, j).start()

        for d in range(2):

            @pl.when(t == RIGHT + d)
            def _():
                for j in range(2):
                    two(0, d, j).start()

        @pl.when(t < 4)
        def _():
            for h in range(2):
                yf_copy(t, h).start()

    def relay(p):
        for j, d in both_ways:
            one(p, d, j).wait_recv()
            low, high = SUBS[j]
            mine = packed[p, RIGHT + d, :, d * half + low : d * half + high].astype(F32)
            three_send[p, d, :, low:high] = (mine + one_recv[p, d, :, low:high].astype(F32)).astype(BF16)
            three(p, d, j).start()

    relay(0)
    for j, d in both_ways:
        one(1, d, j).start()

    @pl.loop(5, 8)
    def _(t):
        pack_to(t)
        for d in range(2):

            @pl.when(t == 4 + RIGHT + d)
            def _():
                for j in range(2):
                    two(1, d, j).start()


    def sum_y(i):
        all_of(yf_recv.at[i], yf_rs.at[i]).wait()
        for h in range(2):
            mine = packed[1, i, :, h * half + X_FIRST : (h + 1) * half].astype(F32)
            t_sum[i, h] = (mine + yf_recv[i, h].astype(F32)).astype(BF16)

    def arrived(p, h, low, high):
        return (
            packed[p, OWN, :, h * half + low : h * half + high].astype(F32)
            + three_recv[p, h, :, low:high].astype(F32)
            + two_recv[p, 1 - h, :, low:high].astype(F32)
        )

    await_all(node_recv, node_rs)
    stacked = node_recv[...].reshape(n_feat * 16, nodes)
    terms[...] = jnp.dot(stacked, masked[...], **HIGH).reshape(terms.shape)
    start_all(terms, terms_recv, term_ss, term_rs)
    terms_recv[f] = terms[f]

    relay(1)

    sum_y(OPP)
    for d in range(2):
        t_one_copy(d).start()
    for d in range(2):
        sum_y(RIGHT + d)
        t_two_copy(d).start()
    for j, h in both_ways:
        two(0, 1 - h, j).wait_recv()
        three(0, h, j).wait_recv()
        y_send[h, :, SUBS[j][0] : SUBS[j][1]] = arrived(0, h, *SUBS[j]).astype(BF16)
        y_copy(h, j).start()
    for d in range(2):
        t_one_copy(d).wait_recv()
        t_three_send[d] = (t_sum[RIGHT + d, d].astype(F32) + t_one[d].astype(F32)).astype(BF16)
        t_three_copy(d).start()

    await_all(terms_recv, term_rs)
    total = terms_recv[0]
    for k in range(1, n_feat):
        total = total + terms_recv[k]
    term[...] = total

    @pl.loop(1, n_edge)
    def _(k):
        peer = lax.rem(e + k, n_edge)
        pltpu.make_async_remote_copy(
            src_ref=term, dst_ref=edge_recv.at[e], send_sem=edge_ss, recv_sem=edge_rs,
            device_id={"edge": peer}, device_id_type=MESH,
        ).start()

    edge_recv[e] = term[...]
    await_all(back_recv, back_rs)

    def finish(h, low, total):
        span, piece = nodes // 2, 512
        for r in range(2):
            for k in range(total.shape[1] // piece):
                node = r * 2 * half + h * half + low + k * piece
                src, part, at = node // nodes, node % nodes // span, node % span
                back = back_recv[src, :, at : at + piece].astype(F32)[part * 8 : part * 8 + 8]
                rows = total[r * 8 : r * 8 + 8, k * piece : (k + 1) * piece]
                out_ref[:, node : node + piece] = (rows + back).astype(BF16)

    for j, h in both_ways:
        low, high = SUBS[j]
        two(1, 1 - h, j).wait_recv()
        three(1, h, j).wait_recv()
        y_copy(h, j).wait_recv()
        finish(h, low, arrived(1, h, low, high) + y_recv[h, :, low:high].astype(F32))
    sum_y(OWN)
    for h in range(2):
        t_two_copy(1 - h).wait_recv()
        t_three_copy(h).wait_recv()
        finish(h, X_FIRST, t_sum[OWN, h].astype(F32) + t_three_recv[h].astype(F32) + t_two[1 - h].astype(F32))

    edge_bytes = edge_recv.at[pl.ds(0, n_edge - 1)]
    all_of(edge_bytes, edge_rs).wait()
    total = edge_recv[0]
    for k in range(1, n_edge):
        total = total + edge_recv[k]
    weight_ref[...] = total * factor

    await_all(back_send, back_ss)
    await_all(node_send, node_ss)
    await_all(terms, term_ss)

    sent = (
        (edge_bytes, edge_ss), (one_recv, one_ss), (two_recv, two_ss), (three_send, three_ss), (y_send, y_ss),
        (yf_recv, yf_ss), (t_one, t_one_ss), (t_two, t_two_ss), (t_three_send, t_three_ss),
    )
    for ref, sem in sent:
        all_of(ref, sem).wait()


def layer(counts, row_index, col_index, w_self, w_neigh, grad_out, pre_act, feat_t, agg_t, blocks, n_feat, n_edge, factor):
    nodes, hidden = grad_out.shape
    features, slab = feat_t.shape
    slots = blocks.shape[0]
    half = slab // 4
    y_first = half - X_FIRST
    names = n_edge * slab // 64
    spots = (slots // 128, 128)
    smem = pl.BlockSpec(memory_space=pltpu.SMEM)
    vmem = pl.BlockSpec(memory_space=pltpu.VMEM)
    hbm = pl.BlockSpec(memory_space=pl.ANY)
    dma = pltpu.SemaphoreType.DMA
    ints = [spots, spots, (2, names // 128, 128)]
    small, large = (n_feat, 16, nodes // 2), (n_feat, 16, nodes)
    x_part = (2, 2, 16, X_FIRST)
    y_part = (2, 16, X_FIRST)
    return pl.pallas_call(
        functools.partial(layer_kernel, n_feat, factor),
        in_specs=[smem, smem] + [hbm] * 9,
        out_specs=[vmem] * 2,
        out_shape=[
            jax.ShapeDtypeStruct((features, slab), BF16),
            jax.ShapeDtypeStruct((2 * features, hidden), F32),
        ],
        scratch_shapes=[
            pltpu.VMEM(w_neigh.shape, BF16),
            pltpu.VMEM((nodes, hidden), BF16),
            pltpu.VMEM((nodes, hidden), BF16),
            pltpu.VMEM(spots, jnp.int32),
            pltpu.VMEM(spots, jnp.int32),
            pltpu.VMEM(w_self.shape, BF16),
            pltpu.VMEM((features, slab), BF16),
            pltpu.VMEM((features, slab), BF16),
            pltpu.VMEM(blocks.shape, BF16),
            pltpu.VMEM((nodes, hidden), BF16),
            pltpu.VMEM((128, 1024), BF16),
            pltpu.VMEM((slab // 64, 16, 256), BF16),
            pltpu.VMEM((slots // 2 + 1, 8, 128), F32),
            pltpu.VMEM((slots // 2 + 1, 8, 128), F32),
            pltpu.VMEM((256, 128), F32),
            pltpu.VMEM((256, 128), F32),
            pltpu.VMEM((2, 4, 16, 2 * half), BF16),
            *[pltpu.VMEM(i, jnp.int32) for i in ints],
            *[pltpu.SMEM(i, jnp.int32) for i in ints],
            *[pltpu.VMEM(i, BF16) for i in (small, small, small, small, large, large)],
            pltpu.VMEM((n_feat, 16, hidden), F32),
            pltpu.VMEM((n_feat, 16, hidden), F32),
            pltpu.VMEM((16, hidden), F32),
            pltpu.VMEM((n_edge, 16, hidden), F32),
            *[pltpu.VMEM(i, BF16) for i in (x_part, x_part, x_part, x_part, y_part, y_part)],
            *[pltpu.VMEM((4, 2, 16, y_first), BF16) for i in range(2)],
            *[pltpu.VMEM((2, 16, y_first), BF16) for i in range(4)],
            dma((9,)),
            dma((3,)),
            *[dma] * 10,
            *[dma, dma((2, 2, 2))] * 3,
            *[dma, dma((2, 2))],
            *[dma, dma((4,))],
            *[dma, dma((2,))] * 3,
        ],
        compiler_params=pltpu.CompilerParams(collective_id=0, has_side_effects=True, vmem_limit_bytes=60 * MIB),
        name="layer",
    )(counts, col_index, row_index.reshape(spots), col_index.reshape(spots), w_self, w_neigh, grad_out, pre_act, feat_t, agg_t, blocks)


def split_kernel(out_ref, weight_ref, feat_ref, self_ref, neigh_ref):
    features = out_ref.shape[0]
    feat_ref[...] = out_ref[...]
    self_ref[...] = weight_ref[:features]
    neigh_ref[...] = weight_ref[features:]


def split(out, weights):
    features = out.shape[0]
    weight = jax.ShapeDtypeStruct((features, weights.shape[1]), F32)
    vmem = pl.BlockSpec(memory_space=pltpu.VMEM)
    return pl.pallas_call(
        split_kernel,
        in_specs=[vmem] * 2,
        out_specs=[vmem] * 3,
        out_shape=[jax.ShapeDtypeStruct(out.shape, BF16), weight, weight],
        name="split",
    )(out, weights)


def on_device(grad_out, pre_act, feat_t, agg_t, w_self, w_neigh, blocks, row_index, col_index, counts):
    n_feat = lax.axis_size("feat")
    n_edge = lax.axis_size("edge")
    slab = feat_t.shape[1]
    factor = 1.0 / math.sqrt(slab * n_edge)
    out, weights = layer(
        counts, row_index, col_index, w_self, w_neigh, grad_out, pre_act, feat_t, agg_t, blocks, n_feat, n_edge, factor
    )
    return tuple(split(out, weights))


def solution(mesh):
    in_specs = (
        P(("edge", "feat"), None),
        P(("edge", "feat"), None),
        P("feat", "edge"),
        P("feat", "edge"),
        P(),
        P(),
        P("edge", None),
        P("edge"),
        P("edge"),
        P("edge"),
    )
    out_specs = (P("feat", "edge"), P("feat", None), P("feat", None))
    return jax.shard_map(
        on_device, mesh=mesh, in_specs=in_specs, out_specs=out_specs, check_vma=False
    )
```

```python
import functools
import math

import jax
import jax.numpy as jnp
from jax import lax
from jax.experimental import pallas as pl
from jax.experimental.pallas import tpu as pltpu
from jax.sharding import PartitionSpec as P

MESH = pl.DeviceIdType.MESH
MIB = 2**20
F32 = jnp.float32
BF16 = jnp.bfloat16
HIGH = dict(preferred_element_type=F32)
NT = (((1,), (1,)), ((), ()))


def masked_rows(grad_ref, pre_ref):
    return jnp.where(pre_ref[...] > 0, grad_ref[...], jnp.zeros_like(grad_ref))


def halves_of(product, owner):
    nodes = product.shape[1]
    rows = product[owner * 8 : owner * 8 + 8]
    both = jnp.concatenate([rows[:, : nodes // 2], rows[:, nodes // 2 :]], 0)
    return both.astype(BF16)


def find_chains(count_ref, col_smem, row_ref, col_ref, row_out, prev_out, last_out):
    slots = row_ref.shape[0] * 128
    count = count_ref[0]

    def count_up(shape):
        return lax.broadcasted_iota(jnp.int32, shape, 0) * 128 + lax.broadcasted_iota(jnp.int32, shape, 1)

    spot = count_up(row_ref.shape)
    alive = spot < count
    row_out[...] = jnp.where(alive, row_ref[...], 0)
    cols = [jnp.where(alive & (spot % 2 == k), col_ref[...], -2) for k in range(2)]
    names = count_up(last_out.shape[1:])

    def body(i, carry):
        prev, last = carry[0], list(carry[1:])
        for u in range(32):
            s = i * 32 + u
            place = i * 16 + u // 2
            c = jnp.where(s < count, col_smem[s], -1)
            prev = jnp.where((cols[u % 2] == c) & (spot > s), place, prev)
            last[u % 2] = jnp.where(names == c, place, last[u % 2])
        return prev, *last

    none = [jnp.full(n, slots // 2, jnp.int32) for n in (row_ref.shape, names.shape, names.shape)]
    prev, *last = lax.fori_loop(0, slots // 32, body, tuple(none))
    prev_out[...] = prev
    for k in range(2):
        last_out[k] = last[k]


def build_table(sources, neigh, table, permute_ref):
    tiles = neigh.shape[2] // 128
    x = jnp.concatenate([neigh[i, :, t * 128 : (t + 1) * 128] for i in sources for t in range(tiles)], 0)
    for b in range(2):
        y = jnp.dot(x, permute_ref[:, b * 512 : (b + 1) * 512], **HIGH)
        for n, i in enumerate(sources):
            for t in range(tiles):
                for h in range(2):
                    at = (n * tiles + t) * 16 + h * 8
                    both = jnp.concatenate([y[at : at + 8, :256], y[at : at + 8, 256:]], 0)
                    table[i * (4 * tiles) + h * 2 * tiles + 2 * t + b] = both.astype(BF16)


def permutation():
    place = lax.broadcasted_iota(jnp.int32, (128, 1024), 1)
    source = place // 512 * 64 + (place % 256) // 8 * 2 + place // 256 % 2
    node = lax.broadcasted_iota(jnp.int32, (128, 1024), 0)
    return jnp.where(source == node, 1.0, 0.0).astype(BF16)


def products(row_smem, prev_smem, blocks, table, sums, even, odd):
    slots = blocks.shape[0]
    steps = slots // 128
    lane = lax.broadcasted_iota(jnp.int32, (8, 128), 1)
    own = lax.broadcasted_iota(jnp.int32, (16, 256), 1) % 8
    for k in range(2):
        sums[k][slots // 2] = jnp.zeros((8, 128), F32)

    def product(step, g, dst):
        rows = pl.ds(pl.multiple_of(step * 128 + g * 16, 16), 16)
        tiles = [blocks[rows, t * 128 : (t + 1) * 128].astype(F32) for t in range(32)]
        for h in range(2):
            left = []
            for q in range(8):
                mine = table[row_smem[step, g * 16 + h * 8 + q]]
                left.append(jnp.where(own == q, mine, jnp.zeros((16, 256), BF16)))
            right = jnp.concatenate([t[h * 8 : h * 8 + 8] for t in tiles], 0).astype(BF16)
            dst[h * 128 : h * 128 + 128] = jnp.dot(jnp.concatenate(left, 0), right, **HIGH)

    def collect(step, g, src):
        for q in range(16):
            before = sums[q % 2][prev_smem[step, g * 16 + q]]
            v = jnp.where(lane < 64, src[q * 16 : q * 16 + 8], src[q * 16 + 8 : q * 16 + 16])
            sums[q % 2][step * 64 + g * 8 + q // 2] = v + before

    kept = (even, odd)
    product(0, 0, even)

    @pl.loop(0, steps, unroll=2)
    def _(step):
        for g in range(8):
            if g < 7:
                product(step, g + 1, kept[(g + 1) % 2])
            else:
                product(jnp.minimum(step + 1, steps - 1), 0, even)
            collect(step, g, kept[g % 2])


def pack(e, last_smem, sums, out_ref):
    rows = out_ref.shape[1] // 64 // 128
    lane = lax.broadcasted_iota(jnp.int32, (8, 128), 1)
    for k in range(rows):
        for u in range(64):
            two = []
            for h in range(2):
                r = (e * 2 + h) * rows + k
                a, b = [sums[0][last_smem[0, r, c]] + sums[1][last_smem[1, r, c]] for c in (2 * u, 2 * u + 1)]
                two.append(jnp.where(lane < 64, a, b) + pltpu.roll(jnp.where(lane < 64, b, a), 64, 1))
            low = (k * 64 + u) * 128
            out_ref[:, low : low + 128] = jnp.concatenate(two, 0).astype(BF16)


X_FIRST = 5632
SUBS = ((0, 2560), (2560, 5632))


def layer_kernel(
    n_feat, factor, count_ref, col_smem, row_hbm, col_hbm, w_self_hbm, w_neigh_hbm, grad_hbm, pre_hbm, feat_hbm, agg_hbm,
    blocks_hbm, out_ref, weight_ref,
    w_neigh, grad, pre, row, col, w_self, feat, agg, blocks, masked, permute, table, sums_even, sums_odd, even, odd, packed,
    row_v, prev_v, last_v, row_s, prev_s, last_s,
    neigh_send, neigh, back_send, back_recv, node_send, node_recv, terms, terms_recv, term, edge_recv,
    one_recv, two_recv, three_send, three_recv, y_send, y_recv,
    yf_recv, t_sum, t_one, t_two, t_three_send, t_three_recv,
    load_sem, index_sem, neigh_ss, neigh_rs, back_ss, back_rs, node_ss, node_rs, term_ss, term_rs, edge_ss, edge_rs,
    one_ss, one_rs, two_ss, two_rs, three_ss, three_rs, y_ss, y_rs,
    yf_ss, yf_rs, t_one_ss, t_one_rs, t_two_ss, t_two_rs, t_three_ss, t_three_rs,
):
    f = lax.axis_index("feat")
    e = lax.axis_index("edge")
    x, y = e // 2, e % 2
    n_edge = 8
    sums = (sums_even, sums_odd)
    barrier = pltpu.get_barrier_semaphore()

    @pl.loop(1, n_feat)
    def _(k):
        peer = {"feat": lax.rem(f + k, n_feat)}
        pl.semaphore_signal(barrier, inc=1, device_id=peer, device_id_type=MESH)

    @pl.loop(1, n_edge)
    def _(k):
        peer = {"edge": lax.rem(e + k, n_edge)}
        pl.semaphore_signal(barrier, inc=1, device_id=peer, device_id_type=MESH)

    pairs = (
        (w_neigh_hbm, w_neigh), (grad_hbm, grad), (pre_hbm, pre), (row_hbm, row), (col_hbm, col),
        (w_self_hbm, w_self), (feat_hbm, feat), (agg_hbm, agg), (blocks_hbm, blocks),
    )
    loads = [pltpu.make_async_copy(a, b, load_sem.at[i]) for i, (a, b) in enumerate(pairs)]
    for c in loads[:3]:
        c.start()

    def all_of(ref, sem):
        return pltpu.make_async_copy(ref, ref, sem)

    def start_all(src, dst, send_sem, recv_sem):
        @pl.loop(1, n_feat)
        def _(k):
            peer = lax.rem(f + k, n_feat)
            pltpu.make_async_remote_copy(
                src_ref=src.at[peer], dst_ref=dst.at[f], send_sem=send_sem, recv_sem=recv_sem,
                device_id={"feat": peer}, device_id_type=MESH,
            ).start()

    def await_all(ref, sem):
        all_of(ref.at[pl.ds(0, n_feat - 1)], sem).wait()

    for c in loads[:3]:
        c.wait()
    for c in loads[3:]:
        c.start()
    masked[...] = masked_rows(grad, pre)
    nodes = grad.shape[0]
    product = lax.dot_general(w_neigh[...], masked[...], NT, **HIGH)
    for owner in range(n_feat):
        neigh_send[owner] = halves_of(product, owner)
    pl.semaphore_wait(barrier, n_feat - 1 + n_edge - 1)
    start_all(neigh_send, neigh, neigh_ss, neigh_rs)

    neigh[f] = neigh_send[f]
    permute[...] = permutation()
    loads[3].wait()
    loads[4].wait()
    find_chains(count_ref, col_smem, row, col, row_v, prev_v, last_v)
    places = ((row_v, row_s), (prev_v, prev_s), (last_v, last_s))
    moves = [pltpu.make_async_copy(a, b, index_sem.at[i]) for i, (a, b) in enumerate(places)]
    for c in moves:
        c.start()
    loads[5].wait()
    product = lax.dot_general(w_self[...], masked[...], NT, **HIGH)
    for owner in range(n_feat):
        back_send[owner] = halves_of(product, owner)
    loads[6].wait()
    loads[7].wait()
    for owner in range(n_feat):
        span = slice(owner * nodes, (owner + 1) * nodes)
        both = jnp.concatenate([feat[:, span].astype(F32), agg[:, span].astype(F32)], 0)
        node_send[owner] = both.astype(BF16)
    node_recv[f] = node_send[f]
    back_recv[f] = back_send[f]
    await_all(neigh_send, neigh_ss)
    start_all(node_send, node_recv, node_ss, node_rs)
    start_all(back_send, back_recv, back_ss, back_rs)
    await_all(neigh, neigh_rs)
    for low in range(0, n_feat, 4):
        sources = [lax.rem(f + k, n_feat) for k in range(low, low + 4)]
        build_table(sources, neigh, table, permute)
    for c in moves:
        c.wait()
    loads[8].wait()
    products(row_s, prev_s, blocks, table, sums, even, odd)

    half = packed.shape[3] // 2
    step_of = (1, -1)
    OPP, RIGHT, LEFT, OWN = range(4)

    def edge_at(dx, py):
        return lax.rem(x + dx + 4, 4) * 2 + py

    def along_x(src, dst, send_sem, recv_sem, d):
        return pltpu.make_async_remote_copy(
            src_ref=src, dst_ref=dst, send_sem=send_sem, recv_sem=recv_sem,
            device_id={"edge": edge_at(step_of[d], y)}, device_id_type=MESH,
        )

    def along_y(src, dst, send_sem, recv_sem):
        return pltpu.make_async_remote_copy(
            src_ref=src, dst_ref=dst, send_sem=send_sem, recv_sem=recv_sem,
            device_id={"edge": edge_at(0, 1 - y)}, device_id_type=MESH,
        )

    def lanes_of(h, low, high):
        return pl.ds(h * half + low, high - low)

    def sub(j):
        return pl.ds(SUBS[j][0], SUBS[j][1] - SUBS[j][0])

    def one(p, d, j):
        src = packed.at[p, OPP, :, lanes_of(d, *SUBS[j])]
        return along_x(src, one_recv.at[p, d, :, sub(j)], one_ss, one_rs.at[p, d, j], d)

    def two(p, d, j):
        src = packed.at[p, RIGHT + d, :, lanes_of(1 - d, *SUBS[j])]
        return along_x(src, two_recv.at[p, d, :, sub(j)], two_ss, two_rs.at[p, d, j], d)

    def three(p, d, j):
        return along_x(
            three_send.at[p, d, :, sub(j)], three_recv.at[p, d, :, sub(j)],
            three_ss, three_rs.at[p, d, j], d,
        )

    def y_copy(h, j):
        return along_y(y_send.at[h, :, sub(j)], y_recv.at[h, :, sub(j)], y_ss, y_rs.at[h, j])

    def yf_copy(i, h):
        src = packed.at[0, i, :, lanes_of(h, X_FIRST, half)]
        return along_y(src, yf_recv.at[i, h], yf_ss, yf_rs.at[i])

    def t_one_copy(d):
        return along_x(t_sum.at[OPP, d], t_one.at[d], t_one_ss, t_one_rs.at[d], d)

    def t_two_copy(d):
        return along_x(t_sum.at[RIGHT + d, 1 - d], t_two.at[d], t_two_ss, t_two_rs.at[d], d)

    def t_three_copy(d):
        return along_x(t_three_send.at[d], t_three_recv.at[d], t_three_ss, t_three_rs.at[d], d)

    both_ways = [(j, d) for j in range(2) for d in range(2)]

    def pack_to(t):
        p, i = t // 4, t % 4
        dx = lax.rem(2 + 3 * i + (i // 2) * (3 + 2 * (i % 2)), 4)
        py = (1 - p) * (1 - y) + p * y
        pack(lax.rem(x + dx, 4) * 2 + py, last_s, sums, packed.at[p, i])

    @pl.loop(0, 5)
    def _(t):
        pack_to(t)

        @pl.when(t == OPP)
        def _():
            for j, d in both_ways:
                one(0, d, j).start()

        for d in range(2):

            @pl.when(t == RIGHT + d)
            def _():
                for j in range(2):
                    two(0, d, j).start()

        @pl.when(t < 4)
        def _():
            for h in range(2):
                yf_copy(t, h).start()

    def relay(p):
        for j, d in both_ways:
            one(p, d, j).wait_recv()
            low, high = SUBS[j]
            mine = packed[p, RIGHT + d, :, d * half + low : d * half + high].astype(F32)
            three_send[p, d, :, low:high] = (mine + one_recv[p, d, :, low:high].astype(F32)).astype(BF16)
            three(p, d, j).start()

    relay(0)
    for j, d in both_ways:
        one(1, d, j).start()

    @pl.loop(5, 8)
    def _(t):
        pack_to(t)
        for d in range(2):

            @pl.when(t == 4 + RIGHT + d)
            def _():
                for j in range(2):
                    two(1, d, j).start()


    def sum_y(i):
        all_of(yf_recv.at[i], yf_rs.at[i]).wait()
        for h in range(2):
            mine = packed[1, i, :, h * half + X_FIRST : (h + 1) * half].astype(F32)
            t_sum[i, h] = (mine + yf_recv[i, h].astype(F32)).astype(BF16)

    def arrived(p, h, low, high):
        return (
            packed[p, OWN, :, h * half + low : h * half + high].astype(F32)
            + three_recv[p, h, :, low:high].astype(F32)
            + two_recv[p, 1 - h, :, low:high].astype(F32)
        )

    await_all(node_recv, node_rs)
    stacked = node_recv[...].reshape(n_feat * 16, nodes)
    terms[...] = jnp.dot(stacked, masked[...], **HIGH).reshape(terms.shape)
    start_all(terms, terms_recv, term_ss, term_rs)
    terms_recv[f] = terms[f]

    relay(1)

    sum_y(OPP)
    for d in range(2):
        t_one_copy(d).start()
    for d in range(2):
        sum_y(RIGHT + d)
        t_two_copy(d).start()
    for j, h in both_ways:
        two(0, 1 - h, j).wait_recv()
        three(0, h, j).wait_recv()
        y_send[h, :, SUBS[j][0] : SUBS[j][1]] = arrived(0, h, *SUBS[j]).astype(BF16)
        y_copy(h, j).start()
    for d in range(2):
        t_one_copy(d).wait_recv()
        t_three_send[d] = (t_sum[RIGHT + d, d].astype(F32) + t_one[d].astype(F32)).astype(BF16)
        t_three_copy(d).start()

    await_all(terms_recv, term_rs)
    total = terms_recv[0]
    for k in range(1, n_feat):
        total = total + terms_recv[k]
    term[...] = total

    @pl.loop(1, n_edge)
    def _(k):
        peer = lax.rem(e + k, n_edge)
        pltpu.make_async_remote_copy(
            src_ref=term, dst_ref=edge_recv.at[e], send_sem=edge_ss, recv_sem=edge_rs,
            device_id={"edge": peer}, device_id_type=MESH,
        ).start()

    edge_recv[e] = term[...]
    await_all(back_recv, back_rs)

    def finish(h, low, total):
        span, piece = nodes // 2, 512
        for r in range(2):
            for k in range(total.shape[1] // piece):
                node = r * 2 * half + h * half + low + k * piece
                src, part, at = node // nodes, node % nodes // span, node % span
                back = back_recv[src, :, at : at + piece].astype(F32)[part * 8 : part * 8 + 8]
                rows = total[r * 8 : r * 8 + 8, k * piece : (k + 1) * piece]
                out_ref[:, node : node + piece] = (rows + back).astype(BF16)

    for j, h in both_ways:
        low, high = SUBS[j]
        two(1, 1 - h, j).wait_recv()
        three(1, h, j).wait_recv()
        y_copy(h, j).wait_recv()
        finish(h, low, arrived(1, h, low, high) + y_recv[h, :, low:high].astype(F32))
    sum_y(OWN)
    for h in range(2):
        t_two_copy(1 - h).wait_recv()
        t_three_copy(h).wait_recv()
        finish(h, X_FIRST, t_sum[OWN, h].astype(F32) + t_three_recv[h].astype(F32) + t_two[1 - h].astype(F32))

    edge_bytes = edge_recv.at[pl.ds(0, n_edge - 1)]
    all_of(edge_bytes, edge_rs).wait()
    total = edge_recv[0]
    for k in range(1, n_edge):
        total = total + edge_recv[k]
    weight_ref[...] = total * factor

    await_all(back_send, back_ss)
    await_all(node_send, node_ss)
    await_all(terms, term_ss)

    sent = (
        (edge_bytes, edge_ss), (one_recv, one_ss), (two_recv, two_ss), (three_send, three_ss), (y_send, y_ss),
        (yf_recv, yf_ss), (t_one, t_one_ss), (t_two, t_two_ss), (t_three_send, t_three_ss),
    )
    for ref, sem in sent:
        all_of(ref, sem).wait()


def layer(counts, row_index, col_index, w_self, w_neigh, grad_out, pre_act, feat_t, agg_t, blocks, n_feat, n_edge, factor):
    nodes, hidden = grad_out.shape
    features, slab = feat_t.shape
    slots = blocks.shape[0]
    half = slab // 4
    y_first = half - X_FIRST
    names = n_edge * slab // 64
    spots = (slots // 128, 128)
    smem = pl.BlockSpec(memory_space=pltpu.SMEM)
    vmem = pl.BlockSpec(memory_space=pltpu.VMEM)
    hbm = pl.BlockSpec(memory_space=pl.ANY)
    dma = pltpu.SemaphoreType.DMA
    ints = [spots, spots, (2, names // 128, 128)]
    small, large = (n_feat, 16, nodes // 2), (n_feat, 16, nodes)
    x_part = (2, 2, 16, X_FIRST)
    y_part = (2, 16, X_FIRST)
    return pl.pallas_call(
        functools.partial(layer_kernel, n_feat, factor),
        in_specs=[smem, smem] + [hbm] * 9,
        out_specs=[vmem] * 2,
        out_shape=[
            jax.ShapeDtypeStruct((features, slab), BF16),
            jax.ShapeDtypeStruct((2 * features, hidden), F32),
        ],
        scratch_shapes=[
            pltpu.VMEM(w_neigh.shape, BF16),
            pltpu.VMEM((nodes, hidden), BF16),
            pltpu.VMEM((nodes, hidden), BF16),
            pltpu.VMEM(spots, jnp.int32),
            pltpu.VMEM(spots, jnp.int32),
            pltpu.VMEM(w_self.shape, BF16),
            pltpu.VMEM((features, slab), BF16),
            pltpu.VMEM((features, slab), BF16),
            pltpu.VMEM(blocks.shape, BF16),
            pltpu.VMEM((nodes, hidden), BF16),
            pltpu.VMEM((128, 1024), BF16),
            pltpu.VMEM((slab // 64, 16, 256), BF16),
            pltpu.VMEM((slots // 2 + 1, 8, 128), F32),
            pltpu.VMEM((slots // 2 + 1, 8, 128), F32),
            pltpu.VMEM((256, 128), F32),
            pltpu.VMEM((256, 128), F32),
            pltpu.VMEM((2, 4, 16, 2 * half), BF16),
            *[pltpu.VMEM(i, jnp.int32) for i in ints],
            *[pltpu.SMEM(i, jnp.int32) for i in ints],
            *[pltpu.VMEM(i, BF16) for i in (small, small, small, small, large, large)],
            pltpu.VMEM((n_feat, 16, hidden), F32),
            pltpu.VMEM((n_feat, 16, hidden), F32),
            pltpu.VMEM((16, hidden), F32),
            pltpu.VMEM((n_edge, 16, hidden), F32),
            *[pltpu.VMEM(i, BF16) for i in (x_part, x_part, x_part, x_part, y_part, y_part)],
            *[pltpu.VMEM((4, 2, 16, y_first), BF16) for i in range(2)],
            *[pltpu.VMEM((2, 16, y_first), BF16) for i in range(4)],
            dma((9,)),
            dma((3,)),
            *[dma] * 10,
            *[dma, dma((2, 2, 2))] * 3,
            *[dma, dma((2, 2))],
            *[dma, dma((4,))],
            *[dma, dma((2,))] * 3,
        ],
        compiler_params=pltpu.CompilerParams(collective_id=0, has_side_effects=True, vmem_limit_bytes=60 * MIB),
        name="layer",
    )(counts, col_index, row_index.reshape(spots), col_index.reshape(spots), w_self, w_neigh, grad_out, pre_act, feat_t, agg_t, blocks)


def split_kernel(out_ref, weight_ref, feat_ref, self_ref, neigh_ref):
    features = out_ref.shape[0]
    feat_ref[...] = out_ref[...]
    self_ref[...] = weight_ref[:features]
    neigh_ref[...] = weight_ref[features:]


def split(out, weights):
    features = out.shape[0]
    weight = jax.ShapeDtypeStruct((features, weights.shape[1]), F32)
    vmem = pl.BlockSpec(memory_space=pltpu.VMEM)
    return pl.pallas_call(
        split_kernel,
        in_specs=[vmem] * 2,
        out_specs=[vmem] * 3,
        out_shape=[jax.ShapeDtypeStruct(out.shape, BF16), weight, weight],
        name="split",
    )(out, weights)


def on_device(grad_out, pre_act, feat_t, agg_t, w_self, w_neigh, blocks, row_index, col_index, counts):
    n_feat = lax.axis_size("feat")
    n_edge = lax.axis_size("edge")
    slab = feat_t.shape[1]
    factor = 1.0 / math.sqrt(slab * n_edge)
    out, weights = layer(
        counts, row_index, col_index, w_self, w_neigh, grad_out, pre_act, feat_t, agg_t, blocks, n_feat, n_edge, factor
    )
    return tuple(split(out, weights))


def solution(mesh):
    in_specs = (
        P(("edge", "feat"), None),
        P(("edge", "feat"), None),
        P("feat", "edge"),
        P("feat", "edge"),
        P(),
        P(),
        P("edge", None),
        P("edge"),
        P("edge"),
        P("edge"),
    )
    out_specs = (P("feat", "edge"), P("feat", None), P("feat", None))
    return jax.shard_map(
        on_device, mesh=mesh, in_specs=in_specs, out_specs=out_specs, check_vma=False
    )
```
